512 devices in a mesh: half: 2 (over x_lo), grid: 8 (over y), dom: 32 (over z, x_hi, core).
Axes of the slice: x: 4 (x_hi: 2, x_lo: 2; x = x_hi * 2 + x_lo), y: 8, z: 8, core: 2. Of those that a mesh axis runs over, the one named last changes fastest.
Arguments:
- grids: float32 [16, 64, 64, 4096], P(('half', 'grid'), 'dom'), may hold values from -0.8 to 0.8
- levels: int32 [16, 4], replicated, may hold values from 4 to 6, as said below
Outputs:
- combined: float32 [16, 64, 64, 4096], P(('half', 'grid'), 'dom')
The draws below stay inside these ranges and needn't reach their ends.
Inputs may be any that keep to these rules, and one draw needn't show every extreme that they name: `levels`: with base b = (4, 5, 5, 5), rows 0 to 7 are b plus, in some order, (2,1,1,0), (2,1,0,1), (2,0,1,1), (1,1,1,1), (1,1,0,0), (1,0,1,0), (1,0,0,1), (0,0,0,0); rows 8 to 15 are b plus, in some order, (2,1,0,0), (2,0,1,0), (2,0,0,1), (1,1,1,0), (1,1,0,1), (1,0,1,1), (2,0,0,0), (1,0,0,0).
All inputs are finite; a program needn't handle non-finite values.
Results may differ from the reference program's by a relative error of at most 0.0003.
Values sent between devices are 32-bit elements; how exact they have to be, the bound alone decides.
A program may use at most 128 MiB of HBM per device.

```python
import jax
import jax.numpy as jnp
import numpy as np
from jax import lax

LEV1 = 6
LEV2 = 6
LEV3 = 6
LEV4 = 6
GRIDS = 16
N1 = 64
N2 = 64
N3 = 64
N4 = 64


def draw_levels(key, part):
    first_key, second_key = jax.random.split(jax.random.fold_in(key, 11), 2)
    first_half = jnp.array([[2, 1, 1, 0], [2, 1, 0, 1], [2, 0, 1, 1], [1, 1, 1, 1], [1, 1, 0, 0], [1, 0, 1, 0], [1, 0, 0, 1], [0, 0, 0, 0]], dtype=jnp.int32)
    second_half = jnp.array([[2, 1, 0, 0], [2, 0, 1, 0], [2, 0, 0, 1], [1, 1, 1, 0], [1, 1, 0, 1], [1, 0, 1, 1], [2, 0, 0, 0], [1, 0, 0, 0]], dtype=jnp.int32)
    first_half = first_half[jax.random.permutation(first_key, 8)]
    second_half = second_half[jax.random.permutation(second_key, 8)]
    lowest = jnp.array([LEV1 - 2, LEV2 - 1, LEV3 - 1, LEV4 - 1], dtype=jnp.int32)
    return (jnp.concatenate([first_half, second_half], axis=0) + lowest[None, :]).astype(jnp.int32)


def block_levels(own_key, dims, cuts, low, high):
    level, own = 1.0, jax.random.fold_in(own_key, 6)
    for position, blocks in cuts:
        draws = jnp.exp(jax.random.uniform(jax.random.fold_in(own, position), (blocks,), jnp.float32, low / len(cuts), high / len(cuts)))
        level = level * jnp.repeat(draws, dims[position] // blocks).reshape([-1 if axis == position else 1 for axis in range(len(dims))])
    return level


def gaussian(rng, extent, scale, reach, cuts=(), held_as=jnp.bfloat16):
    drawn = jax.random.normal(rng, extent, jnp.float32) * scale
    if len(cuts) > 0:
        drawn = block_levels(rng, extent, cuts, -0.22, 0.18) * drawn
    return jnp.clip(drawn, min=-reach, max=reach).astype(held_as)


def setup_inputs(seed: int = 0) -> dict:
    streams_of = jax.random.split(jax.random.key(seed), 3)
    return {
        "grids": gaussian(streams_of[0], (GRIDS, N1, N2, N3 * N4), 0.1, 0.8, ((0, 16), (1, 32)), jnp.float32),
        "levels": draw_levels(jax.random.fold_in(streams_of[2], 71), 0),
    }


HIGH = lax.Precision.HIGHEST
SPANS = (2, 1, 1, 1)


def level_ordering(level):
    points = 2 ** level
    ordering = [0]
    for section in range(1, level + 1):
        stride = 2 ** (level - section)
        ordering.extend(range(stride, points, 2 * stride))
    return np.array(ordering)


def hier_tables(level_top, spread):
    size_top = 2 ** level_top
    forwards = np.zeros((spread + 1, size_top, size_top))
    backwards = np.zeros((spread + 1, size_top, size_top))
    for offset in range(spread + 1):
        level = level_top - spread + offset
        points = 2 ** level
        down_rows = np.eye(points)
        up_rows = np.eye(points)
        for section in range(level, 0, -1):
            stride = 2 ** (level - section)
            odd_points = np.arange(stride, points, 2 * stride)
            down_rows[odd_points] = down_rows[odd_points] - 0.5 * (down_rows[odd_points - stride] + down_rows[(odd_points + stride) % points])
        for section in range(1, level + 1):
            stride = 2 ** (level - section)
            odd_points = np.arange(stride, points, 2 * stride)
            up_rows[odd_points] = up_rows[odd_points] + 0.5 * (up_rows[odd_points - stride] + up_rows[(odd_points + stride) % points])
        ordering = level_ordering(level)
        forwards[offset, :points, :points] = down_rows[ordering]
        backwards[offset, :points, :points] = up_rows[:, ordering]
    return jnp.asarray(forwards, jnp.float32), jnp.asarray(backwards, jnp.float32)


def combination_weights(levels):
    corners = np.array([[(corner >> place) & 1 for place in range(4)] for corner in range(16)], dtype=np.int32)
    parity = 1 - 2 * (corners.sum(axis=1) % 2)
    raised = levels[:, None, :] + jnp.asarray(corners, dtype=jnp.int32)[None, :, :]
    below = jnp.all(raised[:, :, None, :] <= levels[None, None, :, :], axis=3)
    inside = jnp.any(below, axis=2).astype(jnp.int32)
    return jnp.sum(inside * jnp.asarray(parity, dtype=jnp.int32)[None, :], axis=1)


def pick_tables(tables, level_column, level_top, spread):
    shifted = (level_column - (level_top - spread)).astype(jnp.int32)
    onehot = (jnp.arange(spread + 1, dtype=jnp.int32)[None, :] == shifted[:, None]).astype(jnp.float32)
    return jnp.einsum('gs,sij->gij', onehot, tables, precision=HIGH)


def transform(values, matrices):
    values = jnp.einsum('ai,ibcd->abcd', matrices[0], values, precision=HIGH)
    values = jnp.einsum('bi,aicd->abcd', matrices[1], values, precision=HIGH)
    values = jnp.einsum('ci,abid->abcd', matrices[2], values, precision=HIGH)
    values = jnp.einsum('di,abci->abcd', matrices[3], values, precision=HIGH)
    return values


def reference(grids, levels):
    finest = [LEV1, LEV2, LEV3, LEV4]
    table_sets = [hier_tables(finest[axis_index], SPANS[axis_index]) for axis_index in range(4)]
    weights = combination_weights(levels).astype(jnp.float32)

    def accumulate(running, items):
        grid, level_row, weight = items
        matrices = [pick_tables(table_sets[axis_index][0], level_row[axis_index:axis_index + 1], finest[axis_index], SPANS[axis_index])[0] for axis_index in range(4)]
        surplus = transform(grid.reshape(N1, N2, N3, N4), matrices)
        return running + weight * surplus, None

    totals, unused = lax.scan(accumulate, jnp.zeros((N1, N2, N3, N4), jnp.float32), (grids, levels, weights))

    def expand(level_row):
        matrices = [pick_tables(table_sets[axis_index][1], level_row[axis_index:axis_index + 1], finest[axis_index], SPANS[axis_index])[0] for axis_index in range(4)]
        return transform(totals, matrices).reshape(N1, N2, N3 * N4)

    return lax.map(expand, levels)
```

```python
import jax
import jax.numpy as jnp
import numpy as np
from jax import lax
from jax.experimental import pallas as pl
from jax.experimental.pallas import tpu as pltpu
from jax.sharding import PartitionSpec as P

LEV1 = 6
LEV2 = 6
LEV3 = 6
LEV4 = 6
MESH = pl.DeviceIdType.MESH
LOWEST = (LEV1 - 2, LEV2 - 1, LEV3 - 1, LEV4 - 1)


def combination_weights(levels):
    corners = np.array(
        [[corner >> place & 1 for place in range(4)] for corner in range(16)], dtype=np.int32
    )
    parity = 1 - 2 * (corners.sum(axis=1) % 2)
    raised = levels[:, None, :] + jnp.asarray(corners, dtype=jnp.int32)[None, :, :]
    below = jnp.all(raised[:, :, None, :] <= levels[None, None, :, :], axis=3)
    inside = jnp.any(below, axis=2).astype(jnp.int32)
    return jnp.sum(inside * jnp.asarray(parity, dtype=jnp.int32)[None, :], axis=1)


def lift_tables():
    down = np.zeros((2, 64, 64))
    up = np.zeros((2, 64, 64))
    for p in range(32):
        down[0, p, p] = 1
        up[0, p, p] = 1
        after = (p + 1) % 32
        down[1, p, 2 * p] = 1
        down[1, 32 + p, 2 * p + 1] = 1
        down[1, 32 + p, 2 * p] -= 0.5
        down[1, 32 + p, 2 * after] -= 0.5
        up[1, 2 * p, p] = 1
        up[1, 2 * p + 1, 32 + p] = 1
        up[1, 2 * p + 1, p] += 0.5
        up[1, 2 * p + 1, after] += 0.5
    return down, up


def row_tables():
    down, up = lift_tables()
    forward = np.zeros((2, 128, 128))
    backward = np.zeros((2, 128, 128))
    for a in range(2):
        for k in range(64):
            row = (k // 4) * 8 + a * 4 + k % 4
            forward[:, row, a * 64 : a * 64 + 64] = down[:, k, :]
            backward[:, a * 64 : a * 64 + 64, row] = up[:, :, k]
    return jnp.asarray(forward, jnp.bfloat16), jnp.asarray(backward, jnp.bfloat16)


def lane_tables():
    down, up = lift_tables()
    forward = np.zeros((2, 4, 2, 64, 2, 2, 4, 32))
    backward = np.zeros((2, 2, 2, 4, 32, 4, 2, 64))
    for parity in range(2):
        for j in range(4):
            for high in range(2):
                rows = slice(32 * high, 32 * high + 32)
                forward[:, j, parity, :, parity, high, j, :] = down[:, rows, :].transpose(0, 2, 1)
                backward[:, parity, high, j, :, j, parity, :] = up[:, :, rows].transpose(0, 2, 1)
    return (
        jnp.asarray(forward.reshape(2, 512, 512), jnp.bfloat16),
        jnp.asarray(backward.reshape(2, 512, 512), jnp.bfloat16),
    )


def split(values):
    high = values.astype(jnp.bfloat16)
    low = (values - high.astype(jnp.float32)).astype(jnp.bfloat16)
    return high, low


def dot(left, right):
    return jnp.dot(left, right, preferred_element_type=jnp.float32)


def roll_lanes(values):
    return jnp.concatenate(
        [pltpu.roll(values[:, :128], 96, 1), pltpu.roll(values[:, 128:], 96, 1)], axis=1
    )


def forward_kernel(meta_ref, x_ref, lane_ref, row_ref, send_ref, held):
    c_high = meta_ref[1]
    count = 4 + 4 * c_high

    def step(i, _):
        tiles = [
            x_ref[:, pl.ds(pl.multiple_of((i + j * count) * 128, 128), 128)] for j in range(4)
        ]
        high, low = split(jnp.concatenate(tiles, axis=1))
        lane = lane_ref[0]
        out = dot(high, lane) + dot(low, lane)
        held[jnp.where(c_high == 1, i, 2 * i)] = out[:, :256]
        held[jnp.where(c_high == 1, 8 + i, 2 * i + 1)] = out[:, 256:]
        return 0

    lax.fori_loop(0, count, step, 0)

    @pl.when(c_high == 1)
    def _():
        for m in range(8):
            after = held[m + 1] if m < 7 else roll_lanes(held[0])
            held[8 + m] = held[8 + m] - 0.5 * (held[m] + after)

    def rows(i, _):
        high, low = split(held[i])
        row = row_ref[0]
        out = dot(row, high) + dot(row, low)
        c = i // 8
        m = i % 8
        for b in range(2):
            for d in range(2):
                block = b * 4 + c * 2 + d

                @pl.when(meta_ref[12 + block] == 1)
                def _():
                    slot = meta_ref[4 + block]
                    for half in range(2):
                        start = b * 64 + half * 32
                        send_ref[half * 8 + m, slot] = out[
                            start : start + 32, d * 128 : d * 128 + 128
                        ]

        return 0

    lax.fori_loop(0, 8 + 8 * c_high, rows, 0)


def backward_kernel(meta_ref, recv_ref, lane_ref, row_ref, out_ref, held):
    c_high = meta_ref[1]
    count = 4 + 4 * c_high

    @pl.when(meta_ref[3] == 0)
    def _():
        out_ref[...] = jnp.zeros_like(out_ref)

    @pl.when(meta_ref[3] == 1)
    def _():
        def rows(i, _):
            c = i // 8
            m = i % 8
            columns = []
            for d in range(2):
                parts = []
                for b in range(2):
                    block = b * 4 + c * 2 + d
                    slot = meta_ref[4 + block]
                    covered = meta_ref[12 + block] == 1
                    for half in range(2):
                        part = recv_ref[half * 8 + m, slot]
                        parts.append(jnp.where(covered, part, 0.0))
                columns.append(jnp.concatenate(parts, axis=0))
            high, low = split(jnp.concatenate(columns, axis=1))
            row = row_ref[0]
            held[i] = dot(row, high) + dot(row, low)
            return 0

        lax.fori_loop(0, 8 + 8 * c_high, rows, 0)

        @pl.when(c_high == 1)
        def _():
            for m in range(8):
                after = held[m + 1] if m < 7 else roll_lanes(held[0])
                held[8 + m] = held[8 + m] + 0.5 * (held[m] + after)

        def step(i, _):
            even = held[jnp.where(c_high == 1, i, 2 * i)]
            odd = held[jnp.where(c_high == 1, 8 + i, 2 * i + 1)]
            high, low = split(jnp.concatenate([even, odd], axis=1))
            lane = lane_ref[0]
            out = dot(high, lane) + dot(low, lane)
            for j in range(4):
                out_ref[:, pl.ds(pl.multiple_of((i + j * count) * 128, 128), 128)] = out[
                    :, j * 128 : j * 128 + 128
                ]
            return 0

        lax.fori_loop(0, count, step, 0)

        @pl.when(c_high == 0)
        def _():
            out_ref[:, 2048:] = jnp.zeros((128, 2048), jnp.float32)


def exchange_kernel(
    slot_ref,
    coef_ref,
    pick_ref,
    send_ref,
    out_ref,
    r1,
    acc,
    r2,
    o2,
    r3,
    s2,
    send1,
    recv1,
    send2,
    recv2,
    send2c,
    recv2c,
    send3,
    recv3,
    send3c,
    recv3c,
    send4,
    recv4,
    own,
):
    half = lax.axis_index("half")
    me = half * 8 + lax.axis_index("grid")
    dom = lax.axis_index("dom")
    far = dom // 16

    for s in range(8):
        r2[s, 2] = jnp.zeros((8, 128), jnp.float32)

    barrier = pltpu.get_barrier_semaphore()

    def greet_group(k, _):
        peer = (me + k) % 16
        pl.semaphore_signal(
            barrier, inc=1, device_id={"half": peer // 8, "grid": peer % 8}, device_id_type=MESH
        )
        return 0

    def greet_dom(k, _):
        pl.semaphore_signal(
            barrier, inc=1, device_id={"dom": (dom + k) % 32}, device_id_type=MESH
        )
        return 0

    lax.fori_loop(1, 16, greet_group, 0)
    lax.fori_loop(1, 32, greet_dom, 0)
    pl.semaphore_wait(barrier, 46)

    def sized(key, act):
        for option in range(3):

            @pl.when(key == option)
            def _():
                act(8 >> option)

    def copy1(source, peer, count):
        return pltpu.make_async_remote_copy(
            src_ref=send_ref.at[peer, pl.ds(0, count)],
            dst_ref=r1.at[source, pl.ds(0, count)],
            send_sem=send1.at[peer],
            recv_sem=recv1.at[source],
            device_id={"half": peer // 8, "grid": peer % 8},
            device_id_type=MESH,
        )

    def start1(k, _):
        peer = (me + k) % 16
        sized(half + far, lambda count: copy1(me, peer, count).start())
        return 0

    lax.fori_loop(1, 16, start1, 0)

    def wait1(k, _):
        source = (me + 16 - k) % 16
        sized(source // 8 + far, lambda count: copy1(source, source, count).wait_recv())
        return 0

    lax.fori_loop(1, 16, wait1, 0)

    def first(block, _):
        slot = slot_ref[me * 8 + block]
        base = (me * 8 + block) * 3
        for group in range(4):
            value = send_ref[me, slot, pl.ds(group * 8, 8), :]
            for kind in range(3):
                acc[block * 4 + group, kind] = value * coef_ref[base + kind]
        return 0

    lax.fori_loop(0, 8, first, 0)

    def add(i, _):
        source = (me + 1 + i // 8) % 16
        block = i % 8
        slot = slot_ref[source * 8 + block]
        base = (source * 8 + block) * 3
        for group in range(4):
            value = r1[source, slot, pl.ds(group * 8, 8), :]
            for kind in range(3):
                acc[block * 4 + group, kind] += value * coef_ref[base + kind]
        return 0

    lax.fori_loop(0, 120, add, 0)

    def copy2(source, peer, count):
        return pltpu.make_async_remote_copy(
            src_ref=acc.at[peer, pl.ds(0, count)],
            dst_ref=r2.at[source, pl.ds(0, count)],
            send_sem=send2.at[peer],
            recv_sem=recv2.at[source],
            device_id={"dom": peer},
            device_id_type=MESH,
        )

    def copy2c(source, peer):
        return pltpu.make_async_remote_copy(
            src_ref=acc.at[peer, pl.ds(2, 1)],
            dst_ref=r2.at[source, pl.ds(2, 1)],
            send_sem=send2c.at[peer],
            recv_sem=recv2c.at[source],
            device_id={"dom": peer},
            device_id_type=MESH,
        )

    def paired(key, act):
        for option in range(2):

            @pl.when(key == option)
            def _():
                act(2 - option)

    def start2(k, _):
        peer = (dom + k) % 32
        paired(far, lambda count: copy2(dom, peer, count).start())

        @pl.when((dom // 8) + (peer // 4) == 0)
        def _():
            copy2c(dom, peer).start()

        return 0

    lax.fori_loop(1, 32, start2, 0)
    for kind in range(2):
        r2[dom, kind] = acc[dom, kind]

    @pl.when(dom // 4 == 0)
    def _():
        r2[dom, 2] = acc[dom, 2]

    def wait2(k, _):
        source = (dom + 32 - k) % 32
        paired(source // 16, lambda count: copy2(source, source, count).wait_recv())

        @pl.when((source // 8) + (dom // 4) == 0)
        def _():
            copy2c(source, source).wait_recv()

        return 0

    lax.fori_loop(1, 32, wait2, 0)

    def part(ref, kind, p):
        return ref[p // 2, kind, (p % 2) * 4 : (p % 2) * 4 + 4, :]

    def put(ref, kind, p, value):
        ref[p // 2, kind, (p % 2) * 4 : (p % 2) * 4 + 4, :] = value

    def joined(p):
        p = p % 32
        return part(r2, 0, 2 * p) + part(r2, 1, p)

    def coarse(q):
        q = q % 16
        return joined(2 * q) + part(r2, 2, q)

    for q in range(16):
        here = coarse(q)
        after = coarse(q + 1)
        middle = joined(2 * q + 1) - 0.5 * (joined(2 * q) + joined(2 * q + 2))
        put(o2, 2, q, here)
        put(o2, 1, 2 * q, here)
        put(o2, 1, 2 * q + 1, middle + 0.5 * (here + after))
    for s in range(32):
        here = part(o2, 1, s)
        after = part(o2, 1, (s + 1) % 32)
        fine = part(r2, 0, 2 * s + 1) - 0.5 * (
            part(r2, 0, 2 * s) + part(r2, 0, (2 * s + 2) % 64)
        )
        put(o2, 0, 2 * s, here)
        put(o2, 0, 2 * s + 1, fine + 0.5 * (here + after))

    def copy3(source, peer, count):
        return pltpu.make_async_remote_copy(
            src_ref=o2.at[peer, pl.ds(0, count)],
            dst_ref=r3.at[pl.ds(source * 3, count)],
            send_sem=send3.at[peer],
            recv_sem=recv3.at[source],
            device_id={"dom": peer},
            device_id_type=MESH,
        )

    def copy3c(source, peer):
        return pltpu.make_async_remote_copy(
            src_ref=o2.at[peer, pl.ds(2, 1)],
            dst_ref=r3.at[pl.ds(source * 3 + 2, 1)],
            send_sem=send3c.at[peer],
            recv_sem=recv3c.at[source],
            device_id={"dom": peer},
            device_id_type=MESH,
        )

    def start3(k, _):
        peer = (dom + k) % 32
        paired(peer // 16, lambda count: copy3(dom, peer, count).start())

        @pl.when((dom // 4) + (peer // 8) == 0)
        def _():
            copy3c(dom, peer).start()

        return 0

    lax.fori_loop(1, 32, start3, 0)
    r3[dom * 3] = o2[dom, 0]

    @pl.when(far == 0)
    def _():
        r3[dom * 3 + 1] = o2[dom, 1]

    @pl.when(dom // 8 == 0)
    def _():
        r3[dom * 3 + 2] = o2[dom, 2]

    def wait3(k, _):
        source = (dom + 32 - k) % 32
        paired(far, lambda count: copy3(source, source, count).wait_recv())

        @pl.when((source // 4) + (dom // 8) == 0)
        def _():
            copy3c(source, source).wait_recv()

        return 0

    lax.fori_loop(1, 32, wait3, 0)

    def fill(peer):
        def one(slot, _):
            pick = pick_ref[peer * 8 + slot]
            for group in range(4):
                s2[peer, slot, pl.ds(group * 8, 8), :] = r3[pick + group * 3]
            return 0

        lax.fori_loop(0, 8, one, 0)

    def copy4(source, peer, count):
        return pltpu.make_async_remote_copy(
            src_ref=s2.at[peer, pl.ds(0, count)],
            dst_ref=out_ref.at[source, pl.ds(0, count)],
            send_sem=send4.at[peer],
            recv_sem=recv4.at[source],
            device_id={"half": peer // 8, "grid": peer % 8},
            device_id_type=MESH,
        )

    def start4(k, _):
        peer = (me + k) % 16
        fill(peer)
        sized(peer // 8 + far, lambda count: copy4(me, peer, count).start())
        return 0

    lax.fori_loop(1, 16, start4, 0)
    fill(me)
    mine = pltpu.make_async_copy(s2.at[me], out_ref.at[me], own)
    mine.start()

    def wait4(k, _):
        source = (me + 16 - k) % 16
        sized(half + far, lambda count: copy4(source, source, count).wait_recv())
        return 0

    lax.fori_loop(1, 16, wait4, 0)
    mine.wait()

    def sent_group(k, _):
        peer = (me + k) % 16
        sized(half + far, lambda count: copy1(me, peer, count).wait_send())
        sized(peer // 8 + far, lambda count: copy4(me, peer, count).wait_send())
        return 0

    lax.fori_loop(1, 16, sent_group, 0)

    def sent_dom(k, _):
        peer = (dom + k) % 32
        paired(far, lambda count: copy2(dom, peer, count).wait_send())
        paired(peer // 16, lambda count: copy3(dom, peer, count).wait_send())

        @pl.when((dom // 8) + (peer // 4) == 0)
        def _():
            copy2c(dom, peer).wait_send()

        @pl.when((dom // 4) + (peer // 8) == 0)
        def _():
            copy3c(dom, peer).wait_send()

        return 0

    lax.fori_loop(1, 32, sent_dom, 0)


def exchange(slots, coefs, picks, packed):
    dma = pltpu.SemaphoreType.DMA
    return pl.pallas_call(
        exchange_kernel,
        out_shape=jax.ShapeDtypeStruct((16, 8, 32, 128), jnp.float32),
        in_specs=[pl.BlockSpec(memory_space=pltpu.SMEM)] * 3
        + [pl.BlockSpec(memory_space=pltpu.VMEM)],
        out_specs=pl.BlockSpec(memory_space=pl.ANY),
        scratch_shapes=[
            pltpu.VMEM((16, 8, 32, 128), jnp.float32),
            pltpu.VMEM((32, 3, 8, 128), jnp.float32),
            pltpu.VMEM((32, 3, 8, 128), jnp.float32),
            pltpu.VMEM((32, 3, 8, 128), jnp.float32),
            pltpu.VMEM((96, 8, 128), jnp.float32),
            pltpu.VMEM((16, 8, 32, 128), jnp.float32),
            dma((16,)),
            dma((16,)),
            dma((32,)),
            dma((32,)),
            dma((32,)),
            dma((32,)),
            dma((32,)),
            dma((32,)),
            dma((32,)),
            dma((32,)),
            dma((16,)),
            dma((16,)),
            dma,
        ],
        compiler_params=pltpu.CompilerParams(
            collective_id=0, has_side_effects=True, vmem_limit_bytes=32 * 2**20
        ),
    )(slots, coefs, picks, packed)


def tables(levels, own, dom):
    offsets = levels - jnp.asarray(LOWEST, dtype=jnp.int32)[None, :]
    first, second, third, fourth = [offsets[:, axis : axis + 1] for axis in range(4)]
    weights = combination_weights(levels)[:, None]
    block = jnp.arange(8, dtype=jnp.int32)[None, :]
    b, c, d = block // 4, block // 2 % 2, block % 2
    covered = (b <= second) & (c <= third) & (d <= fourth)
    slots = jnp.where(covered, (b * (1 + third) + c) * (1 + fourth) + d, 0)
    kind = 2 - first
    reach = (dom < (8 << first)).astype(jnp.int32)
    coefs = (weights * reach * covered.astype(jnp.int32))[:, :, None] * (
        kind[:, :, None] == jnp.arange(3, dtype=jnp.int32)[None, None, :]
    ).astype(jnp.int32)
    d_at = block % (1 + fourth)
    c_at = block // (1 + fourth) % (1 + third)
    b_at = block // ((1 + fourth) * (1 + third))
    chosen = jnp.where(b_at <= second, b_at * 4 + c_at * 2 + d_at, 0)
    picks = chosen * 12 + kind * reach
    meta = jnp.concatenate(
        [second, third, fourth, reach, slots, covered.astype(jnp.int32)], axis=1
    )
    meta = lax.dynamic_slice_in_dim(meta, own, 1, 0).reshape(-1)
    return slots.reshape(-1), coefs.astype(jnp.float32).reshape(-1), picks.reshape(-1), meta


def local_call(kernel, meta, values, block, out_shape, lanes, rows):
    return pl.pallas_call(
        kernel,
        out_shape=jax.ShapeDtypeStruct(out_shape, jnp.float32),
        grid_spec=pltpu.PrefetchScalarGridSpec(
            num_scalar_prefetch=1,
            grid=(1,),
            in_specs=[
                pl.BlockSpec(block, lambda i, meta: (0,) * len(block)),
                pl.BlockSpec((1, 512, 512), lambda i, meta: (meta[2], 0, 0)),
                pl.BlockSpec((1, 128, 128), lambda i, meta: (meta[0], 0, 0)),
            ],
            out_specs=pl.BlockSpec(out_shape, lambda i, meta: (0,) * len(out_shape)),
            scratch_shapes=[pltpu.VMEM((16, 128, 256), jnp.float32)],
        ),
        compiler_params=pltpu.CompilerParams(vmem_limit_bytes=32 * 2**20),
    )(meta, values, lanes, rows)


def per_device(grids, levels):
    own = lax.axis_index("half") * 8 + lax.axis_index("grid")
    slots, coefs, picks, meta = tables(levels, own, lax.axis_index("dom"))
    lane_forward, lane_backward = lane_tables()
    row_forward, row_backward = row_tables()
    packed = local_call(
        forward_kernel,
        meta,
        grids.reshape(128, 4096),
        (128, 4096),
        (16, 8, 32, 128),
        lane_forward,
        row_forward,
    )
    received = exchange(slots, coefs, picks, packed)
    combined = local_call(
        backward_kernel,
        meta,
        received,
        (16, 8, 32, 128),
        (128, 4096),
        lane_backward,
        row_backward,
    )
    return combined.reshape(grids.shape)


def solution(mesh):
    return jax.shard_map(
        per_device,
        mesh=mesh,
        in_specs=(P(("half", "grid"), "dom", None, None), P()),
        out_specs=P(("half", "grid"), "dom", None, None),
        check_vma=False,
    )
```

```python
import jax
import jax.numpy as jnp
import numpy as np
from jax import lax
from jax.experimental import pallas as pl
from jax.experimental.pallas import tpu as pltpu
from jax.sharding import PartitionSpec as P

LEV1 = 6
LEV2 = 6
LEV3 = 6
LEV4 = 6
MESH = pl.DeviceIdType.MESH
LOWEST = (LEV1 - 2, LEV2 - 1, LEV3 - 1, LEV4 - 1)


def lift_tables():
    down = np.zeros((2, 64, 64))
    up = np.zeros((2, 64, 64))
    for p in range(32):
        down[0, p, p] = 1
        up[0, p, p] = 1
        after = (p + 1) % 32
        down[1, p, 2 * p] = 1
        down[1, 32 + p, 2 * p + 1] = 1
        down[1, 32 + p, 2 * p] -= 0.5
        down[1, 32 + p, 2 * after] -= 0.5
        up[1, 2 * p, p] = 1
        up[1, 2 * p + 1, 32 + p] = 1
        up[1, 2 * p + 1, p] += 0.5
        up[1, 2 * p + 1, after] += 0.5
    return down, up


def row_tables():
    down, up = lift_tables()
    forward = np.zeros((2, 128, 128))
    backward = np.zeros((2, 128, 128))
    for a in range(2):
        for k in range(64):
            row = (k // 4) * 8 + a * 4 + k % 4
            forward[:, row, a * 64 : a * 64 + 64] = down[:, k, :]
            backward[:, a * 64 : a * 64 + 64, row] = up[:, :, k]
    return jnp.asarray(forward, jnp.bfloat16), jnp.asarray(backward, jnp.bfloat16)


def lane_tables():
    down, up = lift_tables()
    forward = np.zeros((2, 4, 64, 2, 4, 32))
    backward = np.zeros((2, 2, 4, 32, 4, 64))
    for j in range(4):
        for high in range(2):
            rows = slice(32 * high, 32 * high + 32)
            forward[:, j, :, high, j, :] = down[:, rows, :].transpose(0, 2, 1)
            backward[:, high, j, :, j, :] = up[:, :, rows].transpose(0, 2, 1)
    return (
        jnp.asarray(forward.reshape(2, 256, 256), jnp.bfloat16),
        jnp.asarray(backward.reshape(2, 256, 256), jnp.bfloat16),
    )


def split(values):
    high = values.astype(jnp.bfloat16)
    low = (values - high.astype(jnp.float32)).astype(jnp.bfloat16)
    return high, low


def dot(left, right):
    return jnp.dot(left, right, preferred_element_type=jnp.float32)


def roll_lanes(values):
    return jnp.concatenate(
        [pltpu.roll(values[:, :128], 96, 1), pltpu.roll(values[:, 128:], 96, 1)], axis=1
    )


def swap_halves(first, second):
    front = lax.broadcasted_iota(jnp.int32, first.shape, 1) < 64
    return (
        jnp.where(front, first, pltpu.roll(second, 64, 1)),
        jnp.where(front, pltpu.roll(first, 64, 1), second),
    )


def lanes_product(even, odd, table):
    even_high, even_low = split(even)
    odd_high, odd_low = split(odd)
    out = dot(jnp.concatenate([even_high, even_low, odd_high, odd_low], axis=0), table)
    return out[:128] + out[128:256], out[256:384] + out[384:]


def rows_product(table, values):
    high, low = split(values)
    return dot(table, high) + dot(table, low)


def offsets_of(levels_ref, grid):
    return [levels_ref[grid, axis] - LOWEST[axis] for axis in range(4)]


def cover_of(offsets, b, c, d):
    _, second, third, fourth = offsets
    covered = (1 - b + b * second) * (1 - c + c * third) * (1 - d + d * fourth)
    return covered, covered * ((b * (1 + third) + c) * (1 + fourth) + d)


def own_grid():
    return lax.axis_index("half") * 8 + lax.axis_index("grid")


def forward_kernel(levels_ref, x_ref, lane_ref, row_ref, send_ref, held):
    offsets = offsets_of(levels_ref, own_grid())
    _, b_high, c_high, d_high = offsets
    count = 4 + 4 * c_high
    lane = lane_ref[d_high]
    row = row_ref[b_high]

    def step(i, _):
        t0, t1, t2, t3 = [
            x_ref[:, pl.ds(pl.multiple_of((i + j * count) * 128, 128), 128)] for j in range(4)
        ]
        even01, odd01 = swap_halves(t0, t1)
        even23, odd23 = swap_halves(t2, t3)
        even, odd = lanes_product(
            jnp.concatenate([even01, even23], axis=1),
            jnp.concatenate([odd01, odd23], axis=1),
            lane,
        )
        held[jnp.where(c_high == 1, i, 2 * i)] = even
        held[jnp.where(c_high == 1, 8 + i, 2 * i + 1)] = odd
        return 0

    lax.fori_loop(0, count, step, 0)

    @pl.when(c_high == 1)
    def _():
        for m in range(8):
            after = held[m + 1] if m < 7 else roll_lanes(held[0])
            held[8 + m] = held[8 + m] - 0.5 * (held[m] + after)

    def rows(i, _):
        out = rows_product(row, held[i])
        c = i // 8
        m = i % 8
        for b in range(2):
            for d in range(2):
                covered, slot = cover_of(offsets, b, c, d)

                @pl.when(covered == 1)
                def _():
                    for half in range(2):
                        start = b * 64 + half * 32
                        send_ref[half * 8 + m, slot] = out[
                            start : start + 32, d * 128 : d * 128 + 128
                        ]

        return 0

    lax.fori_loop(0, 8 + 8 * c_high, rows, 0)


def backward_kernel(levels_ref, recv_ref, lane_ref, row_ref, out_ref, held):
    offsets = offsets_of(levels_ref, own_grid())
    first, b_high, c_high, d_high = offsets
    count = 4 + 4 * c_high
    inside = lax.axis_index("dom") < lax.shift_left(8, first)

    @pl.when(jnp.logical_not(inside))
    def _():
        out_ref[...] = jnp.zeros_like(out_ref)

    @pl.when(inside)
    def _():
        lane = lane_ref[d_high]
        row = row_ref[b_high]

        def rows(i, _):
            c = i // 8
            m = i % 8
            columns = []
            for d in range(2):
                parts = []
                for b in range(2):
                    covered, slot = cover_of(offsets, b, c, d)
                    for half in range(2):
                        part = recv_ref[half * 8 + m, slot]
                        parts.append(jnp.where(covered == 1, part, 0.0))
                columns.append(jnp.concatenate(parts, axis=0))
            held[i] = rows_product(row, jnp.concatenate(columns, axis=1))
            return 0

        lax.fori_loop(0, 8 + 8 * c_high, rows, 0)

        @pl.when(c_high == 1)
        def _():
            for m in range(8):
                after = held[m + 1] if m < 7 else roll_lanes(held[0])
                held[8 + m] = held[8 + m] + 0.5 * (held[m] + after)

        def step(i, _):
            even, odd = lanes_product(
                held[jnp.where(c_high == 1, i, 2 * i)],
                held[jnp.where(c_high == 1, 8 + i, 2 * i + 1)],
                lane,
            )
            tiles = swap_halves(even[:, :128], odd[:, :128]) + swap_halves(
                even[:, 128:], odd[:, 128:]
            )
            for j in range(4):
                out_ref[:, pl.ds(pl.multiple_of((i + j * count) * 128, 128), 128)] = tiles[j]
            return 0

        lax.fori_loop(0, count, step, 0)

        @pl.when(c_high == 0)
        def _():
            out_ref[:, 2048:] = jnp.zeros((128, 2048), jnp.float32)


def weigh(levels_ref, weight_ref):
    guard = 0x8888
    packed = []
    for grid in range(16):
        first, second, third, fourth = offsets_of(levels_ref, grid)
        packed.append(first + 16 * second + 256 * third + 4096 * fourth)
    rows = lax.broadcasted_iota(jnp.int32, (16, 128), 0)
    corner = lax.broadcasted_iota(jnp.int32, (16, 128), 1)
    bits = [lax.shift_right_logical(corner, place) & 1 for place in range(4)]
    raised = bits[0] + 16 * bits[1] + 256 * bits[2] + 4096 * bits[3]
    for grid in range(16):
        raised = raised + jnp.where(rows == grid, packed[grid], 0)
    count = jnp.zeros((16, 128), jnp.int32)
    for grid in range(16):
        above = ((packed[grid] + guard) - raised) & guard
        count = count + jnp.where(above == guard, 1, 0)
    parity = 1 - 2 * ((bits[0] + bits[1] + bits[2] + bits[3]) & 1)
    signed = jnp.where((count > 0) & (corner < 16), parity, 0).astype(jnp.float32)
    total = jnp.sum(signed, axis=1, keepdims=True)
    weight_ref[...] = jnp.broadcast_to(total, (16, 128))


def exchange_kernel(
    levels_ref,
    send_ref,
    out_ref,
    r1a,
    r1b,
    acca,
    accb,
    r2,
    o2,
    r3a,
    r3b,
    s2,
    weight_ref,
    slot_ref,
    coef_ref,
    pick_ref,
    send1,
    recv1,
    send2,
    recv2,
    send3,
    recv3,
    send4,
    recv4,
    own,
):
    half = lax.axis_index("half")
    me = own_grid()
    dom = lax.axis_index("dom")
    far = dom // 16
    r1 = (r1a, r1b)
    acc = (acca, accb)
    r3 = (r3a, r3b)

    for s in range(8):
        r2[s, 2] = jnp.zeros((8, 128), jnp.float32)

    barrier = pltpu.get_barrier_semaphore()

    def greet_group(k, _):
        peer = (me + k) % 16
        pl.semaphore_signal(
            barrier, inc=1, device_id={"half": peer // 8, "grid": peer % 8}, device_id_type=MESH
        )
        return 0

    def greet_dom(k, _):
        pl.semaphore_signal(
            barrier, inc=1, device_id={"dom": (dom + k) % 32}, device_id_type=MESH
        )
        return 0

    lax.fori_loop(1, 16, greet_group, 0)
    lax.fori_loop(1, 32, greet_dom, 0)
    pl.semaphore_wait(barrier, 46)

    def sized(key, act):
        for option in range(3):

            @pl.when(key == option)
            def _():
                act(8 >> option)

    def copy1(c, source, peer, count):
        return pltpu.make_async_remote_copy(
            src_ref=send_ref.at[peer, pl.ds(0, count), pl.ds(16 * c, 16)],
            dst_ref=r1[c].at[source, pl.ds(0, count)],
            send_sem=send1.at[c, peer],
            recv_sem=recv1.at[c, source],
            device_id={"half": peer // 8, "grid": peer % 8},
            device_id_type=MESH,
        )

    def start1(k, _):
        peer = (me + k) % 16
        sized(half + far, lambda count: copy1(0, me, peer, count).start())
        return 0

    lax.fori_loop(1, 16, start1, 0)

    weigh(levels_ref, weight_ref)
    near = 1 - far
    nearest = jnp.where(dom < 8, 1, 0)

    def table(i, _):
        grid = i // 8
        place = i % 8
        offsets = offsets_of(levels_ref, grid)
        first, second, third, fourth = offsets
        covered, slot = cover_of(offsets, place // 4, place // 2 % 2, place % 2)
        is_two = jnp.where(first == 2, 1, 0)
        is_one = jnp.where(first == 1, 1, 0) * near
        is_zero = jnp.where(first == 0, 1, 0) * nearest
        slot_ref[i] = slot * (is_two + is_one + is_zero)
        coef_ref[3 * i] = (covered * is_two).astype(jnp.float32)
        coef_ref[3 * i + 1] = (covered * is_one).astype(jnp.float32)
        coef_ref[3 * i + 2] = (covered * is_zero).astype(jnp.float32)
        d_at = (place % 2) * fourth
        rest = place + fourth * (place // 2 - place)
        c_at = (rest % 2) * third
        rest = rest + third * (rest // 2 - rest)
        chosen = jnp.where(rest <= second, rest * 4 + c_at * 2 + d_at, 0)
        pick_ref[i] = chosen * 6 + is_one + 2 * is_zero
        return 0

    lax.fori_loop(0, 128, table, 0)

    def next1(k, _):
        peer = (me + k) % 16

        def act(count):
            copy1(0, me, peer, count).wait_send()
            copy1(1, me, peer, count).start()

        sized(half + far, act)
        return 0

    lax.fori_loop(1, 16, next1, 0)

    def tiered(key, act):
        for option in range(3):

            @pl.when(key == option)
            def _():
                act(1 + option)

    def tiers(low, high):
        return (1 - low // 16) + jnp.where((low // 8) + (high // 4) == 0, 1, 0)

    def owner(c, e):
        return (e // 2) * 4 + 2 * c + e % 2

    def copy2(c, source, e, count):
        return pltpu.make_async_remote_copy(
            src_ref=acc[c].at[e, pl.ds(0, count)],
            dst_ref=r2.at[source, pl.ds(0, count)],
            send_sem=send2.at[c, e],
            recv_sem=recv2.at[source],
            device_id={"dom": owner(c, e)},
            device_id_type=MESH,
        )

    def copy3(c, e, peer, count):
        return pltpu.make_async_remote_copy(
            src_ref=o2.at[peer, pl.ds(0, count)],
            dst_ref=r3[c].at[pl.ds(e * 3, count)],
            send_sem=send3.at[peer],
            recv_sem=recv3.at[c, e],
            device_id={"dom": peer},
            device_id_type=MESH,
        )

    def part(ref, kind, p):
        return ref[p // 2, kind, (p % 2) * 4 : (p % 2) * 4 + 4, :]

    def put(ref, kind, p, value):
        ref[p // 2, kind, (p % 2) * 4 : (p % 2) * 4 + 4, :] = value

    def joined(p):
        p = p % 32
        return part(r2, 0, 2 * p) + part(r2, 1, p)

    def coarse(q):
        q = q % 16
        return joined(2 * q) + part(r2, 2, q)

    def lift():
        for q in range(16):
            here = coarse(q)
            after = coarse(q + 1)
            middle = joined(2 * q + 1) - 0.5 * (joined(2 * q) + joined(2 * q + 2))
            put(o2, 2, q, here)
            put(o2, 1, 2 * q, here)
            put(o2, 1, 2 * q + 1, middle + 0.5 * (here + after))
        for s in range(32):
            here = part(o2, 1, s)
            after = part(o2, 1, (s + 1) % 32)
            fine = part(r2, 0, 2 * s + 1) - 0.5 * (
                part(r2, 0, 2 * s) + part(r2, 0, (2 * s + 2) % 64)
            )
            put(o2, 0, 2 * s, here)
            put(o2, 0, 2 * s + 1, fine + 0.5 * (here + after))

    def copy4(c, source, peer, count):
        return pltpu.make_async_remote_copy(
            src_ref=s2.at[peer, pl.ds(0, count), pl.ds(16 * c, 16)],
            dst_ref=out_ref.at[source, pl.ds(0, count), pl.ds(16 * c, 16)],
            send_sem=send4.at[c, peer],
            recv_sem=recv4.at[c, source],
            device_id={"half": peer // 8, "grid": peer % 8},
            device_id_type=MESH,
        )

    mine = dom // 2 % 2
    my_e = (dom // 4) * 2 + dom % 2

    for c in range(2):

        def wait1(k, _):
            source = (me + 16 - k) % 16
            sized(source // 8 + far, lambda count: copy1(c, source, source, count).wait_recv())
            return 0

        lax.fori_loop(1, 16, wait1, 0)

        def keep(slot, _):
            r1[c][me, slot] = send_ref[me, slot, pl.ds(16 * c, 16), :]
            return 0

        lax.fori_loop(0, 8, keep, 0)

        def add(block, _):
            for group in range(2):
                sums = [jnp.zeros((8, 128), jnp.float32) for _ in range(2)]
                for source in range(16):
                    at = source * 8 + block
                    value = r1[c][source, slot_ref[at], pl.ds(group * 8, 8), :]
                    value = value * weight_ref[pl.ds(source, 1), :]
                    for kind in range(2):
                        sums[kind] = sums[kind] + value * coef_ref[3 * at + kind]
                for kind in range(2):
                    acc[c][block * 2 + group, kind] = sums[kind]
            return 0

        lax.fori_loop(0, 8, add, 0)
        for group in range(2):
            total = jnp.zeros((8, 128), jnp.float32)
            for source in range(16):
                value = r1[c][source, 0, pl.ds(group * 8, 8), :]
                value = value * weight_ref[pl.ds(source, 1), :]
                total = total + value * coef_ref[3 * source * 8 + 2]
            acc[c][group, 2] = total

        def start2(k, _):
            e = (my_e + k) % 16
            peer = owner(c, e)

            @pl.when(peer != dom)
            def _():
                tiered(tiers(dom, peer), lambda count: copy2(c, dom, e, count).start())

            return 0

        lax.fori_loop(0, 16, start2, 0)

        @pl.when(mine == c)
        def _():
            for kind in range(2):
                r2[dom, kind] = acc[c][my_e, kind]

            @pl.when(dom // 4 == 0)
            def _():
                r2[dom, 2] = acc[c][my_e, 2]

            def wait2(k, _):
                source = (dom + 32 - k) % 32
                tiered(
                    tiers(source, dom), lambda count: copy2(c, source, my_e, count).wait_recv()
                )
                return 0

            lax.fori_loop(1, 32, wait2, 0)
            lift()

            def start3(k, _):
                peer = (dom + k) % 32
                tiered(tiers(peer, dom), lambda count: copy3(c, my_e, peer, count).start())
                return 0

            lax.fori_loop(1, 32, start3, 0)
            r3[c][my_e * 3] = o2[dom, 0]

            @pl.when(far == 0)
            def _():
                r3[c][my_e * 3 + 1] = o2[dom, 1]

            @pl.when(dom // 4 == 0)
            def _():
                r3[c][my_e * 3 + 2] = o2[dom, 2]

        def wait3(k, _):
            e = (my_e + 16 - k) % 16
            peer = owner(c, e)

            @pl.when(peer != dom)
            def _():
                tiered(tiers(dom, peer), lambda count: copy3(c, e, dom, count).wait_recv())

            return 0

        lax.fori_loop(0, 16, wait3, 0)

        def fill(peer):
            def one(slot, _):
                pick = pick_ref[peer * 8 + slot]
                for group in range(2):
                    s2[peer, slot, pl.ds(16 * c + group * 8, 8), :] = r3[c][pick + group * 3]
                return 0

            lax.fori_loop(0, 8, one, 0)

        def start4(k, _):
            peer = (me + k) % 16
            fill(peer)
            sized(peer // 8 + far, lambda count: copy4(c, me, peer, count).start())
            return 0

        lax.fori_loop(1, 16, start4, 0)
        fill(me)

    home = pltpu.make_async_copy(s2.at[me], out_ref.at[me], own)
    home.start()

    for c in range(2):

        def wait4(k, _):
            source = (me + 16 - k) % 16
            sized(half + far, lambda count: copy4(c, source, source, count).wait_recv())
            return 0

        lax.fori_loop(1, 16, wait4, 0)

    home.wait()

    def sent_group(k, _):
        peer = (me + k) % 16
        sized(half + far, lambda count: copy1(1, me, peer, count).wait_send())
        for c in range(2):
            sized(peer // 8 + far, lambda count: copy4(c, me, peer, count).wait_send())
        return 0

    lax.fori_loop(1, 16, sent_group, 0)

    for c in range(2):

        def sent2(e, _):
            peer = owner(c, e)

            @pl.when(peer != dom)
            def _():
                tiered(tiers(dom, peer), lambda count: copy2(c, dom, e, count).wait_send())

            return 0

        lax.fori_loop(0, 16, sent2, 0)

    def sent3(k, _):
        peer = (dom + k) % 32
        tiered(tiers(peer, dom), lambda count: copy3(0, my_e, peer, count).wait_send())
        return 0

    lax.fori_loop(1, 32, sent3, 0)


def exchange(levels, packed):
    dma = pltpu.SemaphoreType.DMA
    f32 = jnp.float32
    return pl.pallas_call(
        exchange_kernel,
        out_shape=jax.ShapeDtypeStruct((16, 8, 32, 128), f32),
        in_specs=[
            pl.BlockSpec(memory_space=pltpu.SMEM),
            pl.BlockSpec(memory_space=pltpu.VMEM),
        ],
        out_specs=pl.BlockSpec(memory_space=pl.ANY),
        scratch_shapes=[
            pltpu.VMEM((16, 8, 16, 128), f32),
            pltpu.VMEM((16, 8, 16, 128), f32),
            pltpu.VMEM((16, 3, 8, 128), f32),
            pltpu.VMEM((16, 3, 8, 128), f32),
            pltpu.VMEM((32, 3, 8, 128), f32),
            pltpu.VMEM((32, 3, 8, 128), f32),
            pltpu.VMEM((48, 8, 128), f32),
            pltpu.VMEM((48, 8, 128), f32),
            pltpu.VMEM((16, 8, 32, 128), f32),
            pltpu.VMEM((16, 128), f32),
            pltpu.SMEM((128,), jnp.int32),
            pltpu.SMEM((384,), f32),
            pltpu.SMEM((128,), jnp.int32),
            dma((2, 16)),
            dma((2, 16)),
            dma((2, 16)),
            dma((32,)),
            dma((32,)),
            dma((2, 16)),
            dma((2, 16)),
            dma((2, 16)),
            dma,
        ],
        compiler_params=pltpu.CompilerParams(
            collective_id=0, has_side_effects=True, vmem_limit_bytes=32 * 2**20
        ),
    )(levels, packed)


def local_call(kernel, levels, values, out_shape, lanes, rows):
    return pl.pallas_call(
        kernel,
        out_shape=jax.ShapeDtypeStruct(out_shape, jnp.float32),
        in_specs=[pl.BlockSpec(memory_space=pltpu.SMEM)]
        + [pl.BlockSpec(memory_space=pltpu.VMEM)] * 3,
        out_specs=pl.BlockSpec(memory_space=pltpu.VMEM),
        scratch_shapes=[pltpu.VMEM((16, 128, 256), jnp.float32)],
        compiler_params=pltpu.CompilerParams(vmem_limit_bytes=32 * 2**20),
    )(levels, values, lanes, rows)


def per_device(grids, levels):
    lane_forward, lane_backward = lane_tables()
    row_forward, row_backward = row_tables()
    packed = local_call(
        forward_kernel,
        levels,
        grids.reshape(128, 4096),
        (16, 8, 32, 128),
        lane_forward,
        row_forward,
    )
    received = exchange(levels, packed)
    combined = local_call(
        backward_kernel, levels, received, (128, 4096), lane_backward, row_backward
    )
    return combined.reshape(grids.shape)


def solution(mesh):
    return jax.shard_map(
        per_device,
        mesh=mesh,
        in_specs=(P(("half", "grid"), "dom", None, None), P()),
        out_specs=P(("half", "grid"), "dom", None, None),
        check_vma=False,
    )
```

```python
import jax
import jax.numpy as jnp
from jax import lax
from jax.experimental import pallas as pl
from jax.experimental.pallas import tpu as pltpu
from jax.sharding import PartitionSpec as P

LEV1 = 6
LEV2 = 6
LEV3 = 6
LEV4 = 6
MESH = pl.DeviceIdType.MESH
LOWEST = (LEV1 - 2, LEV2 - 1, LEV3 - 1, LEV4 - 1)


def down_entry(high, h, e, p):
    low = jnp.where(p == e * (1 + high), 1.0, 0.0)
    fine = jnp.where(p == 2 * e + 1, 1.0, 0.0)
    fine = fine - jnp.where((p == 2 * e) | (p == ((2 * e + 2) & 63)), 0.5, 0.0)
    return jnp.where(h == 0, low, fine * high.astype(jnp.float32))


def up_entry(high, h, e, p):
    middle = jnp.where((p == 2 * e + 1) | (p == ((2 * e + 63) & 63)), 0.5, 0.0)
    low = jnp.where(p == e * (1 + high), 1.0, 0.0) + middle * high.astype(jnp.float32)
    fine = jnp.where(p == 2 * e + 1, 1.0, 0.0) * high.astype(jnp.float32)
    return jnp.where(h == 0, low, fine)


def lane_table(entry, high, points_axis):
    point = lax.broadcasted_iota(jnp.int32, (256, 256), points_axis)
    place = lax.broadcasted_iota(jnp.int32, (256, 256), 1 - points_axis)
    value = entry(high, place >> 7, place & 31, point & 63)
    return jnp.where((point >> 6) == ((place >> 5) & 3), value, 0.0).astype(jnp.bfloat16)


def row_table(entry, high, points_axis):
    point = lax.broadcasted_iota(jnp.int32, (128, 128), points_axis)
    place = lax.broadcasted_iota(jnp.int32, (128, 128), 1 - points_axis)
    part = (place >> 3) * 4 + (place & 3)
    value = entry(high, part >> 5, part & 31, point & 63)
    return jnp.where((point >> 6) == ((place >> 2) & 1), value, 0.0).astype(jnp.bfloat16)


def split(values):
    high = values.astype(jnp.bfloat16)
    low = (values - high.astype(jnp.float32)).astype(jnp.bfloat16)
    return high, low


def dot(left, right):
    return jnp.dot(left, right, preferred_element_type=jnp.float32)


def roll_lanes(values):
    return jnp.concatenate(
        [pltpu.roll(values[:, :128], 96, 1), pltpu.roll(values[:, 128:], 96, 1)], axis=1
    )


def swap_halves(first, second):
    front = lax.broadcasted_iota(jnp.int32, first.shape, 1) < 64
    return (
        jnp.where(front, first, pltpu.roll(second, 64, 1)),
        jnp.where(front, pltpu.roll(first, 64, 1), second),
    )


def lanes_product(even, odd, table):
    even_high, even_low = split(even)
    odd_high, odd_low = split(odd)
    out = dot(jnp.concatenate([even_high, even_low, odd_high, odd_low], axis=0), table)
    return out[:128] + out[128:256], out[256:384] + out[384:]


def rows_product(table, values):
    high, low = split(values)
    return dot(table, high) + dot(table, low)


def offsets_of(levels_ref, grid):
    return [levels_ref[axis, grid] - LOWEST[axis] for axis in range(4)]


def cover_of(offsets, b, c, d):
    _, second, third, fourth = offsets
    covered = (1 - b + b * second) * (1 - c + c * third) * (1 - d + d * fourth)
    return covered, covered * ((b * (1 + third) + c) * (1 + fourth) + d)


def own_grid():
    return lax.axis_index("half") * 8 + lax.axis_index("grid")


def forward_kernel(levels_ref, x_ref, send_ref, held):
    offsets = offsets_of(levels_ref, own_grid())
    _, b_high, c_high, d_high = offsets
    lane = lane_table(down_entry, d_high, 0)
    row = row_table(down_entry, b_high, 1)

    def tile(t):
        return x_ref[:, t * 128 : t * 128 + 128]

    def parts(i, count):
        even01, odd01 = swap_halves(tile(i), tile(i + count))
        even23, odd23 = swap_halves(tile(i + 2 * count), tile(i + 3 * count))
        return lanes_product(
            jnp.concatenate([even01, even23], axis=1),
            jnp.concatenate([odd01, odd23], axis=1),
            lane,
        )

    def rows(c, m):
        out = rows_product(row, held[c * 8 + m])
        for b in range(2):
            for d in range(2):
                covered, slot = cover_of(offsets, b, c, d)

                @pl.when(covered == 1)
                def _():
                    for half in range(2):
                        start = b * 64 + half * 32
                        send_ref[half * 8 + m, slot] = out[
                            start : start + 32, d * 128 : d * 128 + 128
                        ]

    @pl.when(c_high == 0)
    def _():
        for i in range(4):
            held[2 * i], held[2 * i + 1] = parts(i, 4)

    @pl.when(c_high == 1)
    def _():
        for i in range(8):
            held[i], held[8 + i] = parts(i, 8)
        for m in range(8):
            after = held[m + 1] if m < 7 else roll_lanes(held[0])
            held[8 + m] = held[8 + m] - 0.5 * (held[m] + after)
        for m in range(8):
            rows(1, m)

    for m in range(8):
        rows(0, m)


def backward_kernel(levels_ref, recv_ref, out_ref, held):
    offsets = offsets_of(levels_ref, own_grid())
    first, b_high, c_high, d_high = offsets
    inside = lax.axis_index("dom") < lax.shift_left(8, first)

    @pl.when(jnp.logical_not(inside))
    def _():
        out_ref[...] = jnp.zeros_like(out_ref)

    @pl.when(inside)
    def _():
        lane = lane_table(up_entry, d_high, 1)
        row = row_table(up_entry, b_high, 0)

        def rows(c, m):
            columns = []
            for d in range(2):
                parts = []
                for b in range(2):
                    covered, slot = cover_of(offsets, b, c, d)
                    for half in range(2):
                        part = recv_ref[half * 8 + m, slot]
                        parts.append(jnp.where(covered == 1, part, 0.0))
                columns.append(jnp.concatenate(parts, axis=0))
            held[c * 8 + m] = rows_product(row, jnp.concatenate(columns, axis=1))

        def step(i, count, even, odd):
            even, odd = lanes_product(even, odd, lane)
            tiles = swap_halves(even[:, :128], odd[:, :128]) + swap_halves(
                even[:, 128:], odd[:, 128:]
            )
            for j in range(4):
                t = i + j * count
                out_ref[:, t * 128 : t * 128 + 128] = tiles[j]

        for m in range(8):
            rows(0, m)

        @pl.when(c_high == 1)
        def _():
            for m in range(8):
                rows(1, m)
            for m in range(8):
                after = held[m + 1] if m < 7 else roll_lanes(held[0])
                step(m, 8, held[m], held[8 + m] + 0.5 * (held[m] + after))

        @pl.when(c_high == 0)
        def _():
            for i in range(4):
                step(i, 4, held[2 * i], held[2 * i + 1])
            out_ref[:, 2048:] = jnp.zeros((128, 2048), jnp.float32)


def weigh(levels_ref, weight_ref):
    guard = 0x8888
    packed = []
    for grid in range(16):
        first, second, third, fourth = offsets_of(levels_ref, grid)
        packed.append(first + 16 * second + 256 * third + 4096 * fourth)
    rows = lax.broadcasted_iota(jnp.int32, (16, 128), 0)
    corner = lax.broadcasted_iota(jnp.int32, (16, 128), 1)
    bits = [lax.shift_right_logical(corner, place) & 1 for place in range(4)]
    raised = bits[0] + 16 * bits[1] + 256 * bits[2] + 4096 * bits[3]
    for grid in range(16):
        raised = raised + jnp.where(rows == grid, packed[grid], 0)
    count = jnp.zeros((16, 128), jnp.int32)
    for grid in range(16):
        above = ((packed[grid] + guard) - raised) & guard
        count = count + jnp.where(above == guard, 1, 0)
    parity = 1 - 2 * ((bits[0] + bits[1] + bits[2] + bits[3]) & 1)
    signed = jnp.where((count > 0) & (corner < 16), parity, 0).astype(jnp.float32)
    total = jnp.sum(signed, axis=1, keepdims=True)
    weight_ref[...] = jnp.broadcast_to(total, (16, 128))


def exchange_kernel(
    levels_ref,
    send_ref,
    out_ref,
    r1a,
    r1b,
    acca,
    accb,
    r2,
    o2,
    r3a,
    r3b,
    s2,
    weight_ref,
    slot_ref,
    coef_ref,
    pick_ref,
    send1,
    recv1,
    send2,
    recv2,
    send3,
    recv3,
    send4,
    recv4,
    own,
    ra,
    rb,
    sendr,
    recvr,
    sendf,
    recvf,
):
    half = lax.axis_index("half")
    me = own_grid()
    dom = lax.axis_index("dom")
    far = dom // 16
    r1 = (r1a, r1b)
    acc = (acca, accb)
    r3 = (r3a, r3b)
    relayed = (ra, rb)
    line = me % 8

    for s in range(8):
        r2[s, 2] = jnp.zeros((8, 128), jnp.float32)

    barrier = pltpu.get_barrier_semaphore()

    def greet_group(k, _):
        peer = (me + k) % 16
        pl.semaphore_signal(
            barrier, inc=1, device_id={"half": peer // 8, "grid": peer % 8}, device_id_type=MESH
        )
        return 0

    def greet_dom(k, _):
        pl.semaphore_signal(
            barrier, inc=1, device_id={"dom": (dom + k) % 32}, device_id_type=MESH
        )
        return 0

    lax.fori_loop(1, 16, greet_group, 0)
    lax.fori_loop(1, 32, greet_dom, 0)
    pl.semaphore_wait(barrier, 46)

    def sized(key, act):
        for option in range(3):

            @pl.when(key == option)
            def _():
                act(8 >> option)

    def copy1(c, source, peer, count):
        return pltpu.make_async_remote_copy(
            src_ref=send_ref.at[peer, pl.ds(0, count), pl.ds(16 * c, 16)],
            dst_ref=r1[c].at[source, pl.ds(0, count)],
            send_sem=send1.at[c, peer],
            recv_sem=recv1.at[c, source],
            device_id={"half": peer // 8, "grid": peer % 8},
            device_id_type=MESH,
        )

    def shared(source_half, across, act):
        key = source_half + far

        @pl.when((key == 0) & across)
        def _():
            act(8)

        @pl.when((key == 0) & jnp.logical_not(across))
        def _():
            act(6)

        @pl.when(key == 1)
        def _():
            act(4)

        @pl.when(key == 2)
        def _():
            act(2)

    def relay(c):
        return pltpu.make_async_remote_copy(
            src_ref=send_ref.at[:, pl.ds(6, 2), pl.ds(16 * c, 16)],
            dst_ref=relayed[c],
            send_sem=sendr.at[c],
            recv_sem=recvr.at[c],
            device_id={"half": 1 - half},
            device_id_type=MESH,
        )

    def forward(c, source, peer):
        return pltpu.make_async_remote_copy(
            src_ref=relayed[c].at[peer],
            dst_ref=r1[c].at[source, pl.ds(6, 2)],
            send_sem=sendf.at[c, peer],
            recv_sem=recvf.at[c, source],
            device_id={"half": peer // 8, "grid": peer % 8},
            device_id_type=MESH,
        )

    gives = half + far == 0
    takes = (half == 1) & (far == 0)

    def pass_on(c):
        @pl.when(takes)
        def _():
            relay(c).wait_recv()

            def one(k, _):
                for side in range(2):
                    forward(c, line, side * 8 + (line + k) % 8).start()
                return 0

            lax.fori_loop(1, 8, one, 0)

    @pl.when(gives)
    def _():
        relay(0).start()

    def start1(k, _):
        peer = (me + k) % 16
        shared(half, peer % 8 == line, lambda count: copy1(0, me, peer, count).start())
        return 0

    lax.fori_loop(1, 16, start1, 0)

    weigh(levels_ref, weight_ref)
    near = 1 - far
    nearest = jnp.where(dom < 8, 1, 0)

    def table(i, _):
        grid = i // 8
        place = i % 8
        offsets = offsets_of(levels_ref, grid)
        first, second, third, fourth = offsets
        covered, slot = cover_of(offsets, place // 4, place // 2 % 2, place % 2)
        is_two = jnp.where(first == 2, 1, 0)
        is_one = jnp.where(first == 1, 1, 0) * near
        is_zero = jnp.where(first == 0, 1, 0) * nearest
        slot_ref[i] = slot * (is_two + is_one + is_zero)
        coef_ref[3 * i] = (covered * is_two).astype(jnp.float32)
        coef_ref[3 * i + 1] = (covered * is_one).astype(jnp.float32)
        coef_ref[3 * i + 2] = (covered * is_zero).astype(jnp.float32)
        d_at = (place % 2) * fourth
        rest = place + fourth * (place // 2 - place)
        c_at = (rest % 2) * third
        rest = rest + third * (rest // 2 - rest)
        chosen = jnp.where(rest <= second, rest * 4 + c_at * 2 + d_at, 0)
        pick_ref[i] = chosen * 6 + is_one + 2 * is_zero
        return 0

    lax.fori_loop(0, 128, table, 0)

    @pl.when(gives)
    def _():
        relay(0).wait_send()
        relay(1).start()

    pass_on(0)

    def next1(k, _):
        peer = (me + k) % 16

        def act(count):
            copy1(0, me, peer, count).wait_send()
            copy1(1, me, peer, count).start()

        shared(half, peer % 8 == line, act)
        return 0

    lax.fori_loop(1, 16, next1, 0)
    pass_on(1)

    def tiered(key, act):
        for option in range(3):

            @pl.when(key == option)
            def _():
                act(1 + option)

    def tiers(low, high):
        return (1 - low // 16) + jnp.where((low // 8) + (high // 4) == 0, 1, 0)

    def owner(c, e):
        return (e // 2) * 4 + 2 * c + e % 2

    def copy2(c, source, e, count):
        return pltpu.make_async_remote_copy(
            src_ref=acc[c].at[e, pl.ds(0, count)],
            dst_ref=r2.at[source, pl.ds(0, count)],
            send_sem=send2.at[c, e],
            recv_sem=recv2.at[source],
            device_id={"dom": owner(c, e)},
            device_id_type=MESH,
        )

    def copy3(c, e, peer, count):
        return pltpu.make_async_remote_copy(
            src_ref=o2.at[peer, pl.ds(0, count)],
            dst_ref=r3[c].at[pl.ds(e * 3, count)],
            send_sem=send3.at[peer],
            recv_sem=recv3.at[c, e],
            device_id={"dom": peer},
            device_id_type=MESH,
        )

    def part(ref, kind, p):
        return ref[p // 2, kind, (p % 2) * 4 : (p % 2) * 4 + 4, :]

    def put(ref, kind, p, value):
        ref[p // 2, kind, (p % 2) * 4 : (p % 2) * 4 + 4, :] = value

    def joined(p):
        p = p % 32
        return part(r2, 0, 2 * p) + part(r2, 1, p)

    def coarse(q):
        q = q % 16
        return joined(2 * q) + part(r2, 2, q)

    def lift():
        for q in range(16):
            here = coarse(q)
            after = coarse(q + 1)
            middle = joined(2 * q + 1) - 0.5 * (joined(2 * q) + joined(2 * q + 2))
            put(o2, 2, q, here)
            put(o2, 1, 2 * q, here)
            put(o2, 1, 2 * q + 1, middle + 0.5 * (here + after))
        for s in range(32):
            here = part(o2, 1, s)
            after = part(o2, 1, (s + 1) % 32)
            fine = part(r2, 0, 2 * s + 1) - 0.5 * (
                part(r2, 0, 2 * s) + part(r2, 0, (2 * s + 2) % 64)
            )
            put(o2, 0, 2 * s, here)
            put(o2, 0, 2 * s + 1, fine + 0.5 * (here + after))

    def copy4(c, source, peer, count):
        return pltpu.make_async_remote_copy(
            src_ref=s2.at[peer, pl.ds(0, count), pl.ds(16 * c, 16)],
            dst_ref=out_ref.at[source, pl.ds(0, count), pl.ds(16 * c, 16)],
            send_sem=send4.at[c, peer],
            recv_sem=recv4.at[c, source],
            device_id={"half": peer // 8, "grid": peer % 8},
            device_id_type=MESH,
        )

    mine = dom // 2 % 2
    my_e = (dom // 4) * 2 + dom % 2

    def arrive(c):
        def wait1(k, _):
            source = (me + 16 - k) % 16
            across = source % 8 == line
            shared(source // 8, across, lambda count: copy1(c, source, source, count).wait_recv())

            @pl.when((source // 8 + far == 0) & jnp.logical_not(across))
            def _():
                forward(c, source % 8, source).wait_recv()

            return 0

        lax.fori_loop(1, 16, wait1, 0)

    def summed(c):
        def keep(slot, _):
            r1[c][me, slot] = send_ref[me, slot, pl.ds(16 * c, 16), :]
            return 0

        lax.fori_loop(0, 8, keep, 0)

        def add(block, _):
            for group in range(2):
                sums = [jnp.zeros((8, 128), jnp.float32) for _ in range(2)]
                for source in range(16):
                    at = source * 8 + block
                    value = r1[c][source, slot_ref[at], pl.ds(group * 8, 8), :]
                    value = value * weight_ref[pl.ds(source, 1), :]
                    for kind in range(2):
                        sums[kind] = sums[kind] + value * coef_ref[3 * at + kind]
                for kind in range(2):
                    acc[c][block * 2 + group, kind] = sums[kind]
            return 0

        lax.fori_loop(0, 8, add, 0)
        for group in range(2):
            total = jnp.zeros((8, 128), jnp.float32)
            for source in range(16):
                value = r1[c][source, 0, pl.ds(group * 8, 8), :]
                value = value * weight_ref[pl.ds(source, 1), :]
                total = total + value * coef_ref[3 * source * 8 + 2]
            acc[c][group, 2] = total

        def start2(k, _):
            e = (my_e + k) % 16
            peer = owner(c, e)

            @pl.when(peer != dom)
            def _():
                tiered(tiers(dom, peer), lambda count: copy2(c, dom, e, count).start())

            return 0

        lax.fori_loop(0, 16, start2, 0)

    def owned(c):
        @pl.when(mine == c)
        def _():
            for kind in range(2):
                r2[dom, kind] = acc[c][my_e, kind]

            @pl.when(dom // 4 == 0)
            def _():
                r2[dom, 2] = acc[c][my_e, 2]

            def wait2(k, _):
                source = (dom + 32 - k) % 32
                tiered(
                    tiers(source, dom), lambda count: copy2(c, source, my_e, count).wait_recv()
                )
                return 0

            lax.fori_loop(1, 32, wait2, 0)
            lift()

            def start3(k, _):
                peer = (dom + k) % 32
                tiered(tiers(peer, dom), lambda count: copy3(c, my_e, peer, count).start())
                return 0

            lax.fori_loop(1, 32, start3, 0)
            r3[c][my_e * 3] = o2[dom, 0]

            @pl.when(far == 0)
            def _():
                r3[c][my_e * 3 + 1] = o2[dom, 1]

            @pl.when(dom // 4 == 0)
            def _():
                r3[c][my_e * 3 + 2] = o2[dom, 2]

    def deliver(c):
        def wait3(k, _):
            e = (my_e + 16 - k) % 16
            peer = owner(c, e)

            @pl.when(peer != dom)
            def _():
                tiered(tiers(dom, peer), lambda count: copy3(c, e, dom, count).wait_recv())

            return 0

        lax.fori_loop(0, 16, wait3, 0)

        def fill(peer):
            def one(slot, _):
                pick = pick_ref[peer * 8 + slot]
                for group in range(2):
                    s2[peer, slot, pl.ds(16 * c + group * 8, 8), :] = r3[c][pick + group * 3]
                return 0

            lax.fori_loop(0, 8, one, 0)

        def start4(k, _):
            peer = (me + k) % 16
            fill(peer)
            sized(peer // 8 + far, lambda count: copy4(c, me, peer, count).start())
            return 0

        lax.fori_loop(1, 16, start4, 0)
        fill(me)

    arrive(0)
    summed(0)
    owned(0)
    arrive(1)
    deliver(0)
    summed(1)
    owned(1)
    deliver(1)

    home = pltpu.make_async_copy(s2.at[me], out_ref.at[me], own)
    home.start()

    for c in range(2):

        def wait4(k, _):
            source = (me + 16 - k) % 16
            sized(half + far, lambda count: copy4(c, source, source, count).wait_recv())
            return 0

        lax.fori_loop(1, 16, wait4, 0)

    home.wait()

    def sent_group(k, _):
        peer = (me + k) % 16
        shared(half, peer % 8 == line, lambda count: copy1(1, me, peer, count).wait_send())
        for c in range(2):
            sized(peer // 8 + far, lambda count: copy4(c, me, peer, count).wait_send())
        return 0

    lax.fori_loop(1, 16, sent_group, 0)

    @pl.when(gives)
    def _():
        relay(1).wait_send()

    @pl.when(takes)
    def _():
        def passed(k, _):
            for c in range(2):
                for side in range(2):
                    forward(c, line, side * 8 + (line + k) % 8).wait_send()
            return 0

        lax.fori_loop(1, 8, passed, 0)

    for c in range(2):

        def sent2(e, _):
            peer = owner(c, e)

            @pl.when(peer != dom)
            def _():
                tiered(tiers(dom, peer), lambda count: copy2(c, dom, e, count).wait_send())

            return 0

        lax.fori_loop(0, 16, sent2, 0)

    def sent3(k, _):
        peer = (dom + k) % 32
        tiered(tiers(peer, dom), lambda count: copy3(0, my_e, peer, count).wait_send())
        return 0

    lax.fori_loop(1, 32, sent3, 0)


def exchange(levels, packed):
    dma = pltpu.SemaphoreType.DMA
    f32 = jnp.float32
    return pl.pallas_call(
        exchange_kernel,
        out_shape=jax.ShapeDtypeStruct((16, 8, 32, 128), f32),
        in_specs=[
            pl.BlockSpec(memory_space=pltpu.SMEM),
            pl.BlockSpec(memory_space=pltpu.VMEM),
        ],
        out_specs=pl.BlockSpec(memory_space=pl.ANY),
        scratch_shapes=[
            pltpu.VMEM((16, 8, 16, 128), f32),
            pltpu.VMEM((16, 8, 16, 128), f32),
            pltpu.VMEM((16, 3, 8, 128), f32),
            pltpu.VMEM((16, 3, 8, 128), f32),
            pltpu.VMEM((32, 3, 8, 128), f32),
            pltpu.VMEM((32, 3, 8, 128), f32),
            pltpu.VMEM((48, 8, 128), f32),
            pltpu.VMEM((48, 8, 128), f32),
            pltpu.VMEM((16, 8, 32, 128), f32),
            pltpu.VMEM((16, 128), f32),
            pltpu.SMEM((128,), jnp.int32),
            pltpu.SMEM((384,), f32),
            pltpu.SMEM((128,), jnp.int32),
            dma((2, 16)),
            dma((2, 16)),
            dma((2, 16)),
            dma((32,)),
            dma((32,)),
            dma((2, 16)),
            dma((2, 16)),
            dma((2, 16)),
            dma,
            pltpu.VMEM((16, 2, 16, 128), f32),
            pltpu.VMEM((16, 2, 16, 128), f32),
            dma((2,)),
            dma((2,)),
            dma((2, 16)),
            dma((2, 8)),
        ],
        compiler_params=pltpu.CompilerParams(
            collective_id=0, has_side_effects=True, vmem_limit_bytes=32 * 2**20
        ),
    )(levels, packed)


def local_call(kernel, levels, values, out_shape):
    return pl.pallas_call(
        kernel,
        out_shape=jax.ShapeDtypeStruct(out_shape, jnp.float32),
        in_specs=[
            pl.BlockSpec(memory_space=pltpu.SMEM),
            pl.BlockSpec(memory_space=pltpu.VMEM),
        ],
        out_specs=pl.BlockSpec(memory_space=pltpu.VMEM),
        scratch_shapes=[pltpu.VMEM((16, 128, 256), jnp.float32)],
        compiler_params=pltpu.CompilerParams(vmem_limit_bytes=32 * 2**20),
    )(levels, values)


def per_device(grids, levels):
    turned = levels.T
    packed = local_call(forward_kernel, turned, grids.reshape(128, 4096), (16, 8, 32, 128))
    received = exchange(turned, packed)
    combined = local_call(backward_kernel, turned, received, (128, 4096))
    return combined.reshape(grids.shape)


def solution(mesh):
    return jax.shard_map(
        per_device,
        mesh=mesh,
        in_specs=(P(("half", "grid"), "dom", None, None), P()),
        out_specs=P(("half", "grid"), "dom", None, None),
        check_vma=False,
    )
```

```python
import jax
import jax.numpy as jnp
from jax import lax
from jax.experimental import pallas as pl
from jax.experimental.pallas import tpu as pltpu
from jax.sharding import PartitionSpec as P

LEV1 = 6
LEV2 = 6
LEV3 = 6
LEV4 = 6
MESH = pl.DeviceIdType.MESH
LOWEST = (LEV1 - 2, LEV2 - 1, LEV3 - 1, LEV4 - 1)


def down_entry(high, h, e, p):
    low = jnp.where(p == e * (1 + high), 1.0, 0.0)
    fine = jnp.where(p == 2 * e + 1, 1.0, 0.0)
    fine = fine - jnp.where((p == 2 * e) | (p == ((2 * e + 2) & 63)), 0.5, 0.0)
    return jnp.where(h == 0, low, fine * high.astype(jnp.float32))


def up_entry(high, h, e, p):
    middle = jnp.where((p == 2 * e + 1) | (p == ((2 * e + 63) & 63)), 0.5, 0.0)
    low = jnp.where(p == e * (1 + high), 1.0, 0.0) + middle * high.astype(jnp.float32)
    fine = jnp.where(p == 2 * e + 1, 1.0, 0.0) * high.astype(jnp.float32)
    return jnp.where(h == 0, low, fine)


def lane_table(entry, high, points_axis):
    point = lax.broadcasted_iota(jnp.int32, (256, 256), points_axis)
    place = lax.broadcasted_iota(jnp.int32, (256, 256), 1 - points_axis)
    value = entry(high, place >> 7, place & 31, point & 63)
    return jnp.where((point >> 6) == ((place >> 5) & 3), value, 0.0).astype(jnp.bfloat16)


def row_table(entry, high, points_axis):
    point = lax.broadcasted_iota(jnp.int32, (128, 128), points_axis)
    place = lax.broadcasted_iota(jnp.int32, (128, 128), 1 - points_axis)
    part = (place >> 3) * 4 + (place & 3)
    value = entry(high, part >> 5, part & 31, point & 63)
    return jnp.where((point >> 6) == ((place >> 2) & 1), value, 0.0).astype(jnp.bfloat16)


def split(values):
    high = values.astype(jnp.bfloat16)
    low = (values - high.astype(jnp.float32)).astype(jnp.bfloat16)
    return high, low


def dot(left, right):
    return jnp.dot(left, right, preferred_element_type=jnp.float32)


def roll_lanes(values):
    return jnp.concatenate(
        [pltpu.roll(values[:, :128], 96, 1), pltpu.roll(values[:, 128:], 96, 1)], axis=1
    )


def swap_halves(first, second):
    front = lax.broadcasted_iota(jnp.int32, first.shape, 1) < 64
    return (
        jnp.where(front, first, pltpu.roll(second, 64, 1)),
        jnp.where(front, pltpu.roll(first, 64, 1), second),
    )


def lanes_product(even, odd, table):
    even_high, even_low = split(even)
    odd_high, odd_low = split(odd)
    out = dot(jnp.concatenate([even_high, even_low, odd_high, odd_low], axis=0), table)
    return out[:128] + out[128:256], out[256:384] + out[384:]


def rows_product(table, values):
    high, low = split(values)
    return dot(table, high) + dot(table, low)


def offsets_of(levels_ref, grid):
    return [levels_ref[axis, grid] - LOWEST[axis] for axis in range(4)]


def cover_of(offsets, b, c, d):
    _, second, third, fourth = offsets
    covered = (1 - b + b * second) * (1 - c + c * third) * (1 - d + d * fourth)
    return covered, covered * ((b * (1 + third) + c) * (1 + fourth) + d)


def own_grid():
    return lax.axis_index("half") * 8 + lax.axis_index("grid")


def forward_kernel(levels_ref, x_ref, send_ref, held):
    offsets = offsets_of(levels_ref, own_grid())
    _, b_high, c_high, d_high = offsets
    lane = lane_table(down_entry, d_high, 0)
    row = row_table(down_entry, b_high, 1)

    def tile(t):
        return x_ref[:, t * 128 : t * 128 + 128]

    def parts(i, count):
        even01, odd01 = swap_halves(tile(i), tile(i + count))
        even23, odd23 = swap_halves(tile(i + 2 * count), tile(i + 3 * count))
        return lanes_product(
            jnp.concatenate([even01, even23], axis=1),
            jnp.concatenate([odd01, odd23], axis=1),
            lane,
        )

    def rows(c, m):
        out = rows_product(row, held[c * 8 + m])
        for b in range(2):
            for d in range(2):
                covered, slot = cover_of(offsets, b, c, d)

                @pl.when(covered == 1)
                def _():
                    for half in range(2):
                        start = b * 64 + half * 32
                        send_ref[half * 8 + m, slot] = out[
                            start : start + 32, d * 128 : d * 128 + 128
                        ]

    @pl.when(c_high == 0)
    def _():
        for i in range(4):
            held[2 * i], held[2 * i + 1] = parts(i, 4)

    @pl.when(c_high == 1)
    def _():
        for i in range(8):
            held[i], held[8 + i] = parts(i, 8)
        for m in range(8):
            after = held[m + 1] if m < 7 else roll_lanes(held[0])
            held[8 + m] = held[8 + m] - 0.5 * (held[m] + after)
        for m in range(8):
            rows(1, m)

    for m in range(8):
        rows(0, m)


def backward_kernel(levels_ref, recv_ref, out_ref, held):
    offsets = offsets_of(levels_ref, own_grid())
    first, b_high, c_high, d_high = offsets
    inside = lax.axis_index("dom") < lax.shift_left(8, first)

    @pl.when(jnp.logical_not(inside))
    def _():
        out_ref[...] = jnp.zeros_like(out_ref)

    @pl.when(inside)
    def _():
        lane = lane_table(up_entry, d_high, 1)
        row = row_table(up_entry, b_high, 0)

        def rows(c, m):
            columns = []
            for d in range(2):
                parts = []
                for b in range(2):
                    covered, slot = cover_of(offsets, b, c, d)
                    for half in range(2):
                        part = recv_ref[half * 8 + m, slot]
                        parts.append(jnp.where(covered == 1, part, 0.0))
                columns.append(jnp.concatenate(parts, axis=0))
            held[c * 8 + m] = rows_product(row, jnp.concatenate(columns, axis=1))

        def step(i, count, even, odd):
            even, odd = lanes_product(even, odd, lane)
            tiles = swap_halves(even[:, :128], odd[:, :128]) + swap_halves(
                even[:, 128:], odd[:, 128:]
            )
            for j in range(4):
                t = i + j * count
                out_ref[:, t * 128 : t * 128 + 128] = tiles[j]

        for m in range(8):
            rows(0, m)

        @pl.when(c_high == 1)
        def _():
            for m in range(8):
                rows(1, m)
            for m in range(8):
                after = held[m + 1] if m < 7 else roll_lanes(held[0])
                step(m, 8, held[m], held[8 + m] + 0.5 * (held[m] + after))

        @pl.when(c_high == 0)
        def _():
            for i in range(4):
                step(i, 4, held[2 * i], held[2 * i + 1])
            out_ref[:, 2048:] = jnp.zeros((128, 2048), jnp.float32)


def weigh(levels_ref, weight_ref):
    guard = 0x8888
    packed = []
    for grid in range(16):
        first, second, third, fourth = offsets_of(levels_ref, grid)
        packed.append(first + 16 * second + 256 * third + 4096 * fourth)
    rows = lax.broadcasted_iota(jnp.int32, (16, 128), 0)
    corner = lax.broadcasted_iota(jnp.int32, (16, 128), 1)
    bits = [lax.shift_right_logical(corner, place) & 1 for place in range(4)]
    raised = bits[0] + 16 * bits[1] + 256 * bits[2] + 4096 * bits[3]
    for grid in range(16):
        raised = raised + jnp.where(rows == grid, packed[grid], 0)
    count = jnp.zeros((16, 128), jnp.int32)
    for grid in range(16):
        above = ((packed[grid] + guard) - raised) & guard
        count = count + jnp.where(above == guard, 1, 0)
    parity = 1 - 2 * ((bits[0] + bits[1] + bits[2] + bits[3]) & 1)
    signed = jnp.where((count > 0) & (corner < 16), parity, 0).astype(jnp.float32)
    total = jnp.sum(signed, axis=1, keepdims=True)
    weight_ref[...] = jnp.broadcast_to(total, (16, 128))


def exchange_kernel(levels_ref, send_ref, out_ref, *scratch):
    (
        r1,
        acc,
        r3,
        first_relay,
        second_relay,
        r2,
        o2,
        s2,
        weight_ref,
        slot_ref,
        coef_ref,
        pick_ref,
        send1,
        recv1,
        send2,
        recv2,
        send3,
        recv3,
        send4,
        recv4,
        sendr,
        recvr,
        sendf,
        recvf,
        own,
    ) = [scratch[4 * i : 4 * i + 4] for i in range(5)] + list(scratch[20:])
    half = lax.axis_index("half")
    line = lax.axis_index("grid")
    me = half * 8 + line
    dom = lax.axis_index("dom")
    far = dom // 16
    twin = dom + 2 - 4 * (dom // 2 % 2)
    mine = dom % 4
    my_e = dom // 4
    relayed = (first_relay, second_relay)

    for s in range(8):
        r2[s, 2] = jnp.zeros((8, 128), jnp.float32)

    barrier = pltpu.get_barrier_semaphore()

    def greet_group(k, _):
        peer = (me + k) % 16
        pl.semaphore_signal(
            barrier, inc=1, device_id={"half": peer // 8, "grid": peer % 8}, device_id_type=MESH
        )
        return 0

    def greet_dom(k, _):
        pl.semaphore_signal(
            barrier, inc=1, device_id={"dom": (dom + k) % 32}, device_id_type=MESH
        )
        return 0

    def greet_twin(k, _):
        pl.semaphore_signal(
            barrier,
            inc=1,
            device_id={"half": 1 - half, "grid": k, "dom": twin},
            device_id_type=MESH,
        )
        return 0

    lax.fori_loop(1, 16, greet_group, 0)
    lax.fori_loop(1, 32, greet_dom, 0)
    lax.fori_loop(0, 8, greet_twin, 0)
    pl.semaphore_wait(barrier, 54)

    def rows(c):
        return pl.ds(8 * c, 8)

    def sized(key, act):
        for option in range(3):

            @pl.when(key == option)
            def _():
                act(8 >> option)

    def copy1(c, source, peer, count):
        return pltpu.make_async_remote_copy(
            src_ref=send_ref.at[peer, pl.ds(0, count), rows(c)],
            dst_ref=r1[c].at[source, pl.ds(0, count)],
            send_sem=send1.at[c, peer],
            recv_sem=recv1.at[c, source],
            device_id={"half": peer // 8, "grid": peer % 8},
            device_id_type=MESH,
        )

    def shared(source_half, across, act):
        key = source_half + far

        @pl.when((key == 0) & across)
        def _():
            act(8)

        @pl.when((key == 0) & jnp.logical_not(across))
        def _():
            act(6)

        @pl.when(key == 1)
        def _():
            act(4)

        @pl.when(key == 2)
        def _():
            act(2)

    def relay(way, c):
        target = {"half": 1 - half} if way == 0 else {"half": 1 - half, "dom": twin}
        return pltpu.make_async_remote_copy(
            src_ref=send_ref.at[pl.ds(8 - 8 * way, 8), pl.ds(6, 2), rows(c)],
            dst_ref=relayed[way][c],
            send_sem=sendr.at[way, c],
            recv_sem=recvr.at[way, c],
            device_id=target,
            device_id_type=MESH,
        )

    def forward(way, c, source, to):
        target = {"grid": to} if way == 0 else {"half": 1 - half, "grid": to, "dom": twin}
        return pltpu.make_async_remote_copy(
            src_ref=relayed[way][c].at[to],
            dst_ref=r1[c].at[source, pl.ds(6, 2)],
            send_sem=sendf.at[way, c, to],
            recv_sem=recvf.at[c, source],
            device_id=target,
            device_id_type=MESH,
        )

    gives = half + far == 0
    takes = (half == 1) & (far == 0)

    def pass_on(c):
        @pl.when(takes)
        def _():
            for way in range(2):
                relay(way, c).wait_recv()

                def one(k, _):
                    forward(way, c, line, (line + k) % 8).start()
                    return 0

                lax.fori_loop(1, 8, one, 0)

    def start1(c):
        def one(k, _):
            peer = (me + k) % 16
            shared(half, peer % 8 == line, lambda count: copy1(c, me, peer, count).start())
            return 0

        lax.fori_loop(1, 16, one, 0)

    @pl.when(gives)
    def _():
        for c in range(4):
            for way in range(2):
                relay(way, c).start()

    start1(0)
    start1(1)

    weigh(levels_ref, weight_ref)
    near = 1 - far
    nearest = jnp.where(dom < 8, 1, 0)

    def table(i, _):
        grid = i // 8
        place = i % 8
        offsets = offsets_of(levels_ref, grid)
        first, second, third, fourth = offsets
        covered, slot = cover_of(offsets, place // 4, place // 2 % 2, place % 2)
        is_two = jnp.where(first == 2, 1, 0)
        is_one = jnp.where(first == 1, 1, 0) * near
        is_zero = jnp.where(first == 0, 1, 0) * nearest
        slot_ref[i] = slot * (is_two + is_one + is_zero)
        coef_ref[3 * i] = (covered * is_two).astype(jnp.float32)
        coef_ref[3 * i + 1] = (covered * is_one).astype(jnp.float32)
        coef_ref[3 * i + 2] = (covered * is_zero).astype(jnp.float32)
        d_at = (place % 2) * fourth
        rest = place + fourth * (place // 2 - place)
        c_at = (rest % 2) * third
        rest = rest + third * (rest // 2 - rest)
        chosen = jnp.where(rest <= second, rest * 4 + c_at * 2 + d_at, 0)
        pick_ref[i] = chosen * 3 + is_one + 2 * is_zero
        return 0

    lax.fori_loop(0, 128, table, 0)

    def tiered(key, act):
        for option in range(3):

            @pl.when(key == option)
            def _():
                act(1 + option)

    def tiers(low, high):
        return (1 - low // 16) + jnp.where((low // 8) + (high // 4) == 0, 1, 0)

    def owner(c, e):
        return 4 * e + c

    def copy2(c, source, e, count):
        return pltpu.make_async_remote_copy(
            src_ref=acc[c].at[e, pl.ds(0, count)],
            dst_ref=r2.at[source, pl.ds(0, count)],
            send_sem=send2.at[c, e],
            recv_sem=recv2.at[source],
            device_id={"dom": owner(c, e)},
            device_id_type=MESH,
        )

    def copy3(c, e, peer, count):
        return pltpu.make_async_remote_copy(
            src_ref=o2.at[peer, pl.ds(0, count)],
            dst_ref=r3[c].at[pl.ds(e * 3, count)],
            send_sem=send3.at[peer],
            recv_sem=recv3.at[c, e],
            device_id={"dom": peer},
            device_id_type=MESH,
        )

    def copy4(c, source, peer, count):
        return pltpu.make_async_remote_copy(
            src_ref=s2.at[peer, pl.ds(0, count), rows(c)],
            dst_ref=out_ref.at[source, pl.ds(0, count), rows(c)],
            send_sem=send4.at[c, peer],
            recv_sem=recv4.at[c, source],
            device_id={"half": peer // 8, "grid": peer % 8},
            device_id_type=MESH,
        )

    def part(ref, kind, p):
        return ref[p // 2, kind, (p % 2) * 4 : (p % 2) * 4 + 4, :]

    def put(ref, kind, p, value):
        ref[p // 2, kind, (p % 2) * 4 : (p % 2) * 4 + 4, :] = value

    def joined(p):
        p = p % 32
        return part(r2, 0, 2 * p) + part(r2, 1, p)

    def coarse(q):
        q = q % 16
        return joined(2 * q) + part(r2, 2, q)

    def lift():
        for q in range(16):
            here = coarse(q)
            after = coarse(q + 1)
            middle = joined(2 * q + 1) - 0.5 * (joined(2 * q) + joined(2 * q + 2))
            put(o2, 2, q, here)
            put(o2, 1, 2 * q, here)
            put(o2, 1, 2 * q + 1, middle + 0.5 * (here + after))
        for s in range(32):
            here = part(o2, 1, s)
            after = part(o2, 1, (s + 1) % 32)
            fine = part(r2, 0, 2 * s + 1) - 0.5 * (
                part(r2, 0, 2 * s) + part(r2, 0, (2 * s + 2) % 64)
            )
            put(o2, 0, 2 * s, here)
            put(o2, 0, 2 * s + 1, fine + 0.5 * (here + after))

    def arrive(c):
        def wait1(k, _):
            source = (me + 16 - k) % 16
            across = source % 8 == line
            shared(source // 8, across, lambda count: copy1(c, source, source, count).wait_recv())

            @pl.when((source // 8 + far == 0) & jnp.logical_not(across))
            def _():
                forward(0, c, source % 8, source % 8).wait_recv()

            return 0

        lax.fori_loop(1, 16, wait1, 0)

    def summed(c):
        def keep(slot, _):
            r1[c][me, slot] = send_ref[me, slot, rows(c), :]
            return 0

        lax.fori_loop(0, 8, keep, 0)

        def add(block, _):
            sums = [jnp.zeros((8, 128), jnp.float32) for _ in range(2)]
            for source in range(16):
                at = source * 8 + block
                value = r1[c][source, slot_ref[at]] * weight_ref[pl.ds(source, 1), :]
                for kind in range(2):
                    sums[kind] = sums[kind] + value * coef_ref[3 * at + kind]
            for kind in range(2):
                acc[c][block, kind] = sums[kind]
            return 0

        lax.fori_loop(0, 8, add, 0)
        total = jnp.zeros((8, 128), jnp.float32)
        for source in range(16):
            value = r1[c][source, 0] * weight_ref[pl.ds(source, 1), :]
            total = total + value * coef_ref[3 * source * 8 + 2]
        acc[c][0, 2] = total

        def start2(k, _):
            e = (my_e + k) % 8
            peer = owner(c, e)

            @pl.when(peer != dom)
            def _():
                tiered(tiers(dom, peer), lambda count: copy2(c, dom, e, count).start())

            return 0

        lax.fori_loop(0, 8, start2, 0)

    def owned(c):
        @pl.when(mine == c)
        def _():
            for kind in range(2):
                r2[dom, kind] = acc[c][my_e, kind]

            @pl.when(my_e == 0)
            def _():
                r2[dom, 2] = acc[c][my_e, 2]

            def wait2(k, _):
                source = (dom + 32 - k) % 32
                tiered(
                    tiers(source, dom), lambda count: copy2(c, source, my_e, count).wait_recv()
                )
                return 0

            lax.fori_loop(1, 32, wait2, 0)
            lift()

            def start3(k, _):
                peer = (dom + k) % 32
                tiered(tiers(peer, dom), lambda count: copy3(c, my_e, peer, count).start())
                return 0

            lax.fori_loop(1, 32, start3, 0)
            r3[c][my_e * 3] = o2[dom, 0]

            @pl.when(far == 0)
            def _():
                r3[c][my_e * 3 + 1] = o2[dom, 1]

            @pl.when(my_e == 0)
            def _():
                r3[c][my_e * 3 + 2] = o2[dom, 2]

    def deliver(c):
        def wait3(k, _):
            e = (my_e + 8 - k) % 8
            peer = owner(c, e)

            @pl.when(peer != dom)
            def _():
                tiered(tiers(dom, peer), lambda count: copy3(c, e, dom, count).wait_recv())

            return 0

        lax.fori_loop(0, 8, wait3, 0)

        def fill(peer):
            for slot in range(8):
                s2[peer, slot, rows(c), :] = r3[c][pick_ref[peer * 8 + slot]]

        def start4(k, _):
            peer = (me + k) % 16
            fill(peer)
            sized(peer // 8 + far, lambda count: copy4(c, me, peer, count).start())
            return 0

        lax.fori_loop(1, 16, start4, 0)
        fill(me)

    pass_on(0)
    pass_on(1)
    arrive(0)
    start1(2)
    summed(0)
    pass_on(2)
    owned(0)
    arrive(1)
    start1(3)
    summed(1)
    pass_on(3)
    owned(1)
    arrive(2)
    summed(2)
    owned(2)
    deliver(0)
    arrive(3)
    summed(3)
    deliver(1)
    owned(3)
    deliver(2)
    deliver(3)

    home = pltpu.make_async_copy(s2.at[me], out_ref.at[me], own)
    home.start()

    for c in range(4):

        def wait4(k, _):
            source = (me + 16 - k) % 16
            sized(half + far, lambda count: copy4(c, source, source, count).wait_recv())
            return 0

        lax.fori_loop(1, 16, wait4, 0)

    home.wait()

    def sent_group(k, _):
        peer = (me + k) % 16
        for c in range(4):
            shared(half, peer % 8 == line, lambda count: copy1(c, me, peer, count).wait_send())
            sized(peer // 8 + far, lambda count: copy4(c, me, peer, count).wait_send())
        return 0

    lax.fori_loop(1, 16, sent_group, 0)

    @pl.when(gives)
    def _():
        for c in range(4):
            for way in range(2):
                relay(way, c).wait_send()

    @pl.when(takes)
    def _():
        def passed(k, _):
            for c in range(4):
                for way in range(2):
                    forward(way, c, line, (line + k) % 8).wait_send()
            return 0

        lax.fori_loop(1, 8, passed, 0)

    for c in range(4):

        def sent2(e, _):
            peer = owner(c, e)

            @pl.when(peer != dom)
            def _():
                tiered(tiers(dom, peer), lambda count: copy2(c, dom, e, count).wait_send())

            return 0

        lax.fori_loop(0, 8, sent2, 0)

    def sent3(k, _):
        peer = (dom + k) % 32
        tiered(tiers(peer, dom), lambda count: copy3(0, my_e, peer, count).wait_send())
        return 0

    lax.fori_loop(1, 32, sent3, 0)


def exchange(levels, packed):
    dma = pltpu.SemaphoreType.DMA
    f32 = jnp.float32
    return pl.pallas_call(
        exchange_kernel,
        out_shape=jax.ShapeDtypeStruct((16, 8, 32, 128), f32),
        in_specs=[
            pl.BlockSpec(memory_space=pltpu.SMEM),
            pl.BlockSpec(memory_space=pltpu.VMEM),
        ],
        out_specs=pl.BlockSpec(memory_space=pl.ANY),
        scratch_shapes=[pltpu.VMEM((16, 8, 8, 128), f32)] * 4
        + [pltpu.VMEM((8, 3, 8, 128), f32)] * 4
        + [pltpu.VMEM((24, 8, 128), f32)] * 4
        + [pltpu.VMEM((8, 2, 8, 128), f32)] * 8
        + [
            pltpu.VMEM((32, 3, 8, 128), f32),
            pltpu.VMEM((32, 3, 8, 128), f32),
            pltpu.VMEM((16, 8, 32, 128), f32),
            pltpu.VMEM((16, 128), f32),
            pltpu.SMEM((128,), jnp.int32),
            pltpu.SMEM((384,), f32),
            pltpu.SMEM((128,), jnp.int32),
            dma((4, 16)),
            dma((4, 16)),
            dma((4, 8)),
            dma((32,)),
            dma((32,)),
            dma((4, 8)),
            dma((4, 16)),
            dma((4, 16)),
            dma((2, 4)),
            dma((2, 4)),
            dma((2, 4, 8)),
            dma((4, 8)),
            dma,
        ],
        compiler_params=pltpu.CompilerParams(
            collective_id=0, has_side_effects=True, vmem_limit_bytes=32 * 2**20
        ),
    )(levels, packed)


def local_call(kernel, levels, values, out_shape):
    return pl.pallas_call(
        kernel,
        out_shape=jax.ShapeDtypeStruct(out_shape, jnp.float32),
        in_specs=[
            pl.BlockSpec(memory_space=pltpu.SMEM),
            pl.BlockSpec(memory_space=pltpu.VMEM),
        ],
        out_specs=pl.BlockSpec(memory_space=pltpu.VMEM),
        scratch_shapes=[pltpu.VMEM((16, 128, 256), jnp.float32)],
        compiler_params=pltpu.CompilerParams(vmem_limit_bytes=32 * 2**20),
    )(levels, values)


def per_device(grids, levels):
    turned = levels.T
    packed = local_call(forward_kernel, turned, grids.reshape(128, 4096), (16, 8, 32, 128))
    received = exchange(turned, packed)
    combined = local_call(backward_kernel, turned, received, (128, 4096))
    return combined.reshape(grids.shape)


def solution(mesh):
    return jax.shard_map(
        per_device,
        mesh=mesh,
        in_specs=(P(("half", "grid"), "dom", None, None), P()),
        out_specs=P(("half", "grid"), "dom", None, None),
        check_vma=False,
    )
```

```python
import jax
import jax.numpy as jnp
from jax import lax
from jax.experimental import pallas as pl
from jax.experimental.pallas import tpu as pltpu
from jax.sharding import PartitionSpec as P

LEV1 = 6
LEV2 = 6
LEV3 = 6
LEV4 = 6
MESH = pl.DeviceIdType.MESH
LOWEST = (LEV1 - 2, LEV2 - 1, LEV3 - 1, LEV4 - 1)


def down_entry(high, h, e, p):
    low = jnp.where(p == e * (1 + high), 1.0, 0.0)
    fine = jnp.where(p == 2 * e + 1, 1.0, 0.0)
    fine = fine - jnp.where((p == 2 * e) | (p == ((2 * e + 2) & 63)), 0.5, 0.0)
    return jnp.where(h == 0, low, fine * high.astype(jnp.float32))


def up_entry(high, h, e, p):
    middle = jnp.where((p == 2 * e + 1) | (p == ((2 * e + 63) & 63)), 0.5, 0.0)
    low = jnp.where(p == e * (1 + high), 1.0, 0.0) + middle * high.astype(jnp.float32)
    fine = jnp.where(p == 2 * e + 1, 1.0, 0.0) * high.astype(jnp.float32)
    return jnp.where(h == 0, low, fine)


def lane_table(entry, high, points_axis):
    point = lax.broadcasted_iota(jnp.int32, (256, 256), points_axis)
    place = lax.broadcasted_iota(jnp.int32, (256, 256), 1 - points_axis)
    value = entry(high, place >> 7, place & 31, point & 63)
    return jnp.where((point >> 6) == ((place >> 5) & 3), value, 0.0).astype(jnp.bfloat16)


def row_table(entry, high, points_axis):
    point = lax.broadcasted_iota(jnp.int32, (128, 128), points_axis)
    place = lax.broadcasted_iota(jnp.int32, (128, 128), 1 - points_axis)
    part = (place >> 3) * 4 + (place & 3)
    value = entry(high, part >> 5, part & 31, point & 63)
    return jnp.where((point >> 6) == ((place >> 2) & 1), value, 0.0).astype(jnp.bfloat16)


def split(values):
    high = values.astype(jnp.bfloat16)
    low = (values - high.astype(jnp.float32)).astype(jnp.bfloat16)
    return high, low


def dot(left, right):
    return jnp.dot(left, right, preferred_element_type=jnp.float32)


def roll_lanes(values):
    return jnp.concatenate(
        [pltpu.roll(values[:, :128], 96, 1), pltpu.roll(values[:, 128:], 96, 1)], axis=1
    )


def swap_halves(first, second):
    front = lax.broadcasted_iota(jnp.int32, first.shape, 1) < 64
    return (
        jnp.where(front, first, pltpu.roll(second, 64, 1)),
        jnp.where(front, pltpu.roll(first, 64, 1), second),
    )


def lanes_product(even, odd, table):
    even_high, even_low = split(even)
    odd_high, odd_low = split(odd)
    out = dot(jnp.concatenate([even_high, even_low, odd_high, odd_low], axis=0), table)
    return out[:128] + out[128:256], out[256:384] + out[384:]


def rows_product(table, values):
    high, low = split(values)
    return dot(table, high) + dot(table, low)


def offsets_of(levels_ref, grid):
    return [levels_ref[axis, grid] - LOWEST[axis] for axis in range(4)]


def cover_of(offsets, b, c, d):
    _, second, third, fourth = offsets
    covered = (1 - b + b * second) * (1 - c + c * third) * (1 - d + d * fourth)
    return covered, covered * ((b * (1 + third) + c) * (1 + fourth) + d)


def own_grid():
    return lax.axis_index("half") * 8 + lax.axis_index("grid")


def blocks_of(offsets, slot):
    _, second, third, fourth = offsets
    d_at = (slot % 2) * fourth
    rest = slot + fourth * (slot // 2 - slot)
    c_at = (rest % 2) * third
    rest = rest + third * (rest // 2 - rest)
    return jnp.where(rest <= second, rest * 4 + c_at * 2 + d_at, 0)


def lower(offsets, x_ref, held, blocks_ref):
    _, b_high, c_high, d_high = offsets
    lane = lane_table(down_entry, d_high, 0)
    row = row_table(down_entry, b_high, 1)
    fine = c_high == 1

    def tile(i, j):
        t = i + 8 * j
        u = i % 4 + 4 * j
        return jnp.where(
            fine, x_ref[:, t * 128 : t * 128 + 128], x_ref[:, u * 128 : u * 128 + 128]
        )

    for i in range(8):
        even01, odd01 = swap_halves(tile(i, 0), tile(i, 1))
        even23, odd23 = swap_halves(tile(i, 2), tile(i, 3))
        held[i], held[8 + i] = lanes_product(
            jnp.concatenate([even01, even23], axis=1),
            jnp.concatenate([odd01, odd23], axis=1),
            lane,
        )
    for m in range(7, -1, -1):
        held[16 + m] = jnp.where(fine, held[m], held[m // 2 + 8 * (m % 2)])
    for m in range(8):
        after = held[17 + m] if m < 7 else roll_lanes(held[16])
        held[8 + m] = held[8 + m] - 0.5 * (held[16 + m] + after)
    for c in range(2):
        for m in range(8):
            out = rows_product(row, held[16 - 8 * c + m])
            for b in range(2):
                for d in range(2):
                    for half in range(2):
                        start = b * 64 + half * 32
                        blocks_ref[half * 8 + m, b * 4 + c * 2 + d] = out[
                            start : start + 32, d * 128 : d * 128 + 128
                        ]


def backward_kernel(levels_ref, recv_ref, out_ref, held):
    offsets = offsets_of(levels_ref, own_grid())
    first, b_high, c_high, d_high = offsets
    inside = lax.axis_index("dom") < lax.shift_left(8, first)

    @pl.when(jnp.logical_not(inside))
    def _():
        out_ref[...] = jnp.zeros_like(out_ref)

    @pl.when(inside)
    def _():
        lane = lane_table(up_entry, d_high, 1)
        row = row_table(up_entry, b_high, 0)

        def rows(c, m):
            columns = []
            for d in range(2):
                parts = []
                for b in range(2):
                    covered, slot = cover_of(offsets, b, c, d)
                    for half in range(2):
                        for group in range(4):
                            part = recv_ref[group, half * 8 + m, slot]
                            parts.append(jnp.where(covered == 1, part, 0.0))
                columns.append(jnp.concatenate(parts, axis=0))
            held[c * 8 + m] = rows_product(row, jnp.concatenate(columns, axis=1))

        def step(i, count, even, odd):
            even, odd = lanes_product(even, odd, lane)
            tiles = swap_halves(even[:, :128], odd[:, :128]) + swap_halves(
                even[:, 128:], odd[:, 128:]
            )
            for j in range(4):
                t = i + j * count
                out_ref[:, t * 128 : t * 128 + 128] = tiles[j]

        for m in range(8):
            rows(0, m)

        @pl.when(c_high == 1)
        def _():
            for m in range(8):
                rows(1, m)
            for m in range(8):
                after = held[m + 1] if m < 7 else roll_lanes(held[0])
                step(m, 8, held[m], held[8 + m] + 0.5 * (held[m] + after))

        @pl.when(c_high == 0)
        def _():
            for i in range(4):
                step(i, 4, held[2 * i], held[2 * i + 1])
            out_ref[:, 2048:] = jnp.zeros((128, 2048), jnp.float32)


def weigh(levels_ref, weight_ref):
    guard = 0x8888
    packed = []
    for grid in range(16):
        first, second, third, fourth = offsets_of(levels_ref, grid)
        packed.append(first + 16 * second + 256 * third + 4096 * fourth)
    rows = lax.broadcasted_iota(jnp.int32, (16, 128), 0)
    corner = lax.broadcasted_iota(jnp.int32, (16, 128), 1)
    bits = [lax.shift_right_logical(corner, place) & 1 for place in range(4)]
    raised = bits[0] + 16 * bits[1] + 256 * bits[2] + 4096 * bits[3]
    for grid in range(16):
        raised = raised + jnp.where(rows == grid, packed[grid], 0)
    count = jnp.zeros((16, 128), jnp.int32)
    for grid in range(16):
        above = ((packed[grid] + guard) - raised) & guard
        count = count + jnp.where(above == guard, 1, 0)
    parity = 1 - 2 * ((bits[0] + bits[1] + bits[2] + bits[3]) & 1)
    signed = jnp.where((count > 0) & (corner < 16), parity, 0).astype(jnp.float32)
    total = jnp.sum(signed, axis=1, keepdims=True)
    weight_ref[...] = jnp.broadcast_to(total, (16, 128))


def exchange_kernel(levels_ref, x_ref, out_ref, *scratch):
    (
        r1,
        acc,
        r3,
        first_relay,
        second_relay,
        r2,
        o2,
        s2,
        weight_ref,
        slot_ref,
        coef_ref,
        pick_ref,
        send1,
        recv1,
        send2,
        recv2,
        send3,
        recv3,
        send4,
        recv4,
        sendr,
        recvr,
        sendf,
        recvf,
        own,
        send_ref,
        held,
        blocks_ref,
    ) = [scratch[4 * i : 4 * i + 4] for i in range(5)] + list(scratch[20:])
    half = lax.axis_index("half")
    line = lax.axis_index("grid")
    me = half * 8 + line
    dom = lax.axis_index("dom")
    far = dom // 16
    twin = dom + 2 - 4 * (dom // 2 % 2)
    mine = dom % 4
    my_e = dom // 4
    relayed = (first_relay, second_relay)

    for s in range(8):
        r2[s, 2] = jnp.zeros((8, 128), jnp.float32)

    barrier = pltpu.get_barrier_semaphore()

    def greet_group(k, _):
        peer = (me + k) % 16
        pl.semaphore_signal(
            barrier, inc=1, device_id={"half": peer // 8, "grid": peer % 8}, device_id_type=MESH
        )
        return 0

    def greet_dom(k, _):
        pl.semaphore_signal(
            barrier, inc=1, device_id={"dom": (dom + k) % 32}, device_id_type=MESH
        )
        return 0

    def greet_twin(k, _):
        pl.semaphore_signal(
            barrier,
            inc=1,
            device_id={"half": 1 - half, "grid": k, "dom": twin},
            device_id_type=MESH,
        )
        return 0

    lax.fori_loop(1, 16, greet_group, 0)
    lax.fori_loop(1, 32, greet_dom, 0)
    lax.fori_loop(0, 8, greet_twin, 0)
    offsets = offsets_of(levels_ref, me)
    lower(offsets, x_ref, held, blocks_ref)
    places = [blocks_of(offsets, slot) for slot in range(8)]

    def pack(c):
        def one(target, _):
            for slot in range(8):
                send_ref[c, target, slot] = blocks_ref[target, places[slot], pl.ds(8 * c, 8), :]
            return 0

        lax.fori_loop(0, 16, one, 0)

    pack(0)
    pl.semaphore_wait(barrier, 54)

    def sized(key, act):
        for option in range(3):

            @pl.when(key == option)
            def _():
                act(8 >> option)

    def copy1(c, source, peer, count):
        return pltpu.make_async_remote_copy(
            src_ref=send_ref.at[c, peer, pl.ds(0, count)],
            dst_ref=r1[c].at[source, pl.ds(0, count)],
            send_sem=send1.at[c, peer],
            recv_sem=recv1.at[c, source],
            device_id={"half": peer // 8, "grid": peer % 8},
            device_id_type=MESH,
        )

    def shared(source_half, across, act):
        key = source_half + far

        @pl.when((key == 0) & across)
        def _():
            act(8)

        @pl.when((key == 0) & jnp.logical_not(across))
        def _():
            act(6)

        @pl.when(key == 1)
        def _():
            act(4)

        @pl.when(key == 2)
        def _():
            act(2)

    def relay(way, c):
        target = {"half": 1 - half} if way == 0 else {"half": 1 - half, "dom": twin}
        return pltpu.make_async_remote_copy(
            src_ref=send_ref.at[c, pl.ds(8 - 8 * way, 8), pl.ds(6, 2)],
            dst_ref=relayed[way][c],
            send_sem=sendr.at[way, c],
            recv_sem=recvr.at[way, c],
            device_id=target,
            device_id_type=MESH,
        )

    def forward(way, c, source, to):
        target = {"grid": to} if way == 0 else {"half": 1 - half, "grid": to, "dom": twin}
        return pltpu.make_async_remote_copy(
            src_ref=relayed[way][c].at[to],
            dst_ref=r1[c].at[source, pl.ds(6, 2)],
            send_sem=sendf.at[way, c, to],
            recv_sem=recvf.at[c, source],
            device_id=target,
            device_id_type=MESH,
        )

    gives = half + far == 0
    takes = (half == 1) & (far == 0)

    def pass_on(c):
        @pl.when(takes)
        def _():
            for way in range(2):
                relay(way, c).wait_recv()

                def one(k, _):
                    forward(way, c, line, (line + k) % 8).start()
                    return 0

                lax.fori_loop(1, 8, one, 0)

    def start1(c):
        def one(k, _):
            peer = (me + k) % 16
            shared(half, peer % 8 == line, lambda count: copy1(c, me, peer, count).start())
            return 0

        lax.fori_loop(1, 16, one, 0)

    def send(c):
        @pl.when(gives)
        def _():
            for way in range(2):
                relay(way, c).start()

        start1(c)

    send(0)
    pack(1)
    send(1)
    pack(2)
    pack(3)

    @pl.when(gives)
    def _():
        for c in range(2, 4):
            for way in range(2):
                relay(way, c).start()

    weigh(levels_ref, weight_ref)
    near = 1 - far
    nearest = jnp.where(dom < 8, 1, 0)

    def table(i, _):
        grid = i // 8
        place = i % 8
        offsets = offsets_of(levels_ref, grid)
        first = offsets[0]
        covered, slot = cover_of(offsets, place // 4, place // 2 % 2, place % 2)
        is_two = jnp.where(first == 2, 1, 0)
        is_one = jnp.where(first == 1, 1, 0) * near
        is_zero = jnp.where(first == 0, 1, 0) * nearest
        slot_ref[i] = slot * (is_two + is_one + is_zero)
        coef_ref[3 * i] = (covered * is_two).astype(jnp.float32)
        coef_ref[3 * i + 1] = (covered * is_one).astype(jnp.float32)
        coef_ref[3 * i + 2] = (covered * is_zero).astype(jnp.float32)
        chosen = blocks_of(offsets, place)
        pick_ref[i] = chosen * 3 + is_one + 2 * is_zero
        return 0

    lax.fori_loop(0, 128, table, 0)

    def tiered(key, act):
        for option in range(3):

            @pl.when(key == option)
            def _():
                act(1 + option)

    def tiers(low, high):
        return (1 - low // 16) + jnp.where((low // 8) + (high // 4) == 0, 1, 0)

    def owner(c, e):
        return 4 * e + c

    def copy2(c, source, e, count):
        return pltpu.make_async_remote_copy(
            src_ref=acc[c].at[e, pl.ds(0, count)],
            dst_ref=r2.at[source, pl.ds(0, count)],
            send_sem=send2.at[c, e],
            recv_sem=recv2.at[source],
            device_id={"dom": owner(c, e)},
            device_id_type=MESH,
        )

    def copy3(c, e, peer, count):
        return pltpu.make_async_remote_copy(
            src_ref=o2.at[peer, pl.ds(0, count)],
            dst_ref=r3[c].at[pl.ds(e * 3, count)],
            send_sem=send3.at[peer],
            recv_sem=recv3.at[c, e],
            device_id={"dom": peer},
            device_id_type=MESH,
        )

    def copy4(c, source, peer, count):
        return pltpu.make_async_remote_copy(
            src_ref=s2.at[c, peer, pl.ds(0, count)],
            dst_ref=out_ref.at[c, source, pl.ds(0, count)],
            send_sem=send4.at[c, peer],
            recv_sem=recv4.at[c, source],
            device_id={"half": peer // 8, "grid": peer % 8},
            device_id_type=MESH,
        )

    def part(ref, kind, p):
        return ref[p // 2, kind, (p % 2) * 4 : (p % 2) * 4 + 4, :]

    def put(ref, kind, p, value):
        ref[p // 2, kind, (p % 2) * 4 : (p % 2) * 4 + 4, :] = value

    def joined(p):
        p = p % 32
        return part(r2, 0, 2 * p) + part(r2, 1, p)

    def coarse(q):
        q = q % 16
        return joined(2 * q) + part(r2, 2, q)

    def lift():
        for q in range(16):
            here = coarse(q)
            after = coarse(q + 1)
            middle = joined(2 * q + 1) - 0.5 * (joined(2 * q) + joined(2 * q + 2))
            put(o2, 2, q, here)
            put(o2, 1, 2 * q, here)
            put(o2, 1, 2 * q + 1, middle + 0.5 * (here + after))
        for s in range(32):
            here = part(o2, 1, s)
            after = part(o2, 1, (s + 1) % 32)
            fine = part(r2, 0, 2 * s + 1) - 0.5 * (
                part(r2, 0, 2 * s) + part(r2, 0, (2 * s + 2) % 64)
            )
            put(o2, 0, 2 * s, here)
            put(o2, 0, 2 * s + 1, fine + 0.5 * (here + after))

    def arrive(c):
        def wait1(k, _):
            source = (me + 16 - k) % 16
            across = source % 8 == line
            shared(source // 8, across, lambda count: copy1(c, source, source, count).wait_recv())

            @pl.when((source // 8 + far == 0) & jnp.logical_not(across))
            def _():
                forward(0, c, source % 8, source % 8).wait_recv()

            return 0

        lax.fori_loop(1, 16, wait1, 0)

    def summed(c):
        def keep(slot, _):
            r1[c][me, slot] = send_ref[c, me, slot]
            return 0

        lax.fori_loop(0, 8, keep, 0)

        def add(block, _):
            sums = [jnp.zeros((8, 128), jnp.float32) for _ in range(2)]
            for source in range(16):
                at = source * 8 + block
                value = r1[c][source, slot_ref[at]] * weight_ref[pl.ds(source, 1), :]
                for kind in range(2):
                    sums[kind] = sums[kind] + value * coef_ref[3 * at + kind]
            for kind in range(2):
                acc[c][block, kind] = sums[kind]
            return 0

        lax.fori_loop(0, 8, add, 0)
        total = jnp.zeros((8, 128), jnp.float32)
        for source in range(16):
            value = r1[c][source, 0] * weight_ref[pl.ds(source, 1), :]
            total = total + value * coef_ref[3 * source * 8 + 2]
        acc[c][0, 2] = total

        def start2(k, _):
            e = (my_e + k) % 8
            peer = owner(c, e)

            @pl.when(peer != dom)
            def _():
                tiered(tiers(dom, peer), lambda count: copy2(c, dom, e, count).start())

            return 0

        lax.fori_loop(0, 8, start2, 0)

    def owned(c):
        @pl.when(mine == c)
        def _():
            for kind in range(2):
                r2[dom, kind] = acc[c][my_e, kind]

            @pl.when(my_e == 0)
            def _():
                r2[dom, 2] = acc[c][my_e, 2]

            def wait2(k, _):
                source = (dom + 32 - k) % 32
                tiered(
                    tiers(source, dom), lambda count: copy2(c, source, my_e, count).wait_recv()
                )
                return 0

            lax.fori_loop(1, 32, wait2, 0)
            lift()

            def start3(k, _):
                peer = (dom + k) % 32
                tiered(tiers(peer, dom), lambda count: copy3(c, my_e, peer, count).start())
                return 0

            lax.fori_loop(1, 32, start3, 0)
            r3[c][my_e * 3] = o2[dom, 0]

            @pl.when(far == 0)
            def _():
                r3[c][my_e * 3 + 1] = o2[dom, 1]

            @pl.when(my_e == 0)
            def _():
                r3[c][my_e * 3 + 2] = o2[dom, 2]

    def deliver(c):
        def wait3(k, _):
            e = (my_e + 8 - k) % 8
            peer = owner(c, e)

            @pl.when(peer != dom)
            def _():
                tiered(tiers(dom, peer), lambda count: copy3(c, e, dom, count).wait_recv())

            return 0

        lax.fori_loop(0, 8, wait3, 0)

        def fill(peer):
            for slot in range(8):
                s2[c, peer, slot] = r3[c][pick_ref[peer * 8 + slot]]

        def start4(k, _):
            peer = (me + k) % 16
            fill(peer)
            sized(peer // 8 + far, lambda count: copy4(c, me, peer, count).start())
            return 0

        lax.fori_loop(1, 16, start4, 0)
        fill(me)

    pass_on(0)
    pass_on(1)
    arrive(0)
    start1(2)
    summed(0)
    pass_on(2)
    owned(0)
    arrive(1)
    start1(3)
    summed(1)
    pass_on(3)
    owned(1)
    arrive(2)
    summed(2)
    owned(2)
    deliver(0)
    arrive(3)
    summed(3)
    deliver(1)
    owned(3)
    deliver(2)
    deliver(3)

    home = pltpu.make_async_copy(s2.at[:, me], out_ref.at[:, me], own)
    home.start()

    for c in range(4):

        def wait4(k, _):
            source = (me + 16 - k) % 16
            sized(half + far, lambda count: copy4(c, source, source, count).wait_recv())
            return 0

        lax.fori_loop(1, 16, wait4, 0)

    home.wait()

    def sent_group(k, _):
        peer = (me + k) % 16
        for c in range(4):
            shared(half, peer % 8 == line, lambda count: copy1(c, me, peer, count).wait_send())
            sized(peer // 8 + far, lambda count: copy4(c, me, peer, count).wait_send())
        return 0

    lax.fori_loop(1, 16, sent_group, 0)

    @pl.when(gives)
    def _():
        for c in range(4):
            for way in range(2):
                relay(way, c).wait_send()

    @pl.when(takes)
    def _():
        def passed(k, _):
            for c in range(4):
                for way in range(2):
                    forward(way, c, line, (line + k) % 8).wait_send()
            return 0

        lax.fori_loop(1, 8, passed, 0)

    for c in range(4):

        def sent2(e, _):
            peer = owner(c, e)

            @pl.when(peer != dom)
            def _():
                tiered(tiers(dom, peer), lambda count: copy2(c, dom, e, count).wait_send())

            return 0

        lax.fori_loop(0, 8, sent2, 0)

    def sent3(k, _):
        peer = (dom + k) % 32
        tiered(tiers(peer, dom), lambda count: copy3(0, my_e, peer, count).wait_send())
        return 0

    lax.fori_loop(1, 32, sent3, 0)


def exchange(levels, values):
    dma = pltpu.SemaphoreType.DMA
    f32 = jnp.float32
    return pl.pallas_call(
        exchange_kernel,
        out_shape=jax.ShapeDtypeStruct((4, 16, 8, 8, 128), f32),
        in_specs=[
            pl.BlockSpec(memory_space=pltpu.SMEM),
            pl.BlockSpec(memory_space=pltpu.VMEM),
        ],
        out_specs=pl.BlockSpec(memory_space=pl.ANY),
        scratch_shapes=[pltpu.VMEM((16, 8, 8, 128), f32)] * 4
        + [pltpu.VMEM((8, 3, 8, 128), f32)] * 4
        + [pltpu.VMEM((24, 8, 128), f32)] * 4
        + [pltpu.VMEM((8, 2, 8, 128), f32)] * 8
        + [
            pltpu.VMEM((32, 3, 8, 128), f32),
            pltpu.VMEM((32, 3, 8, 128), f32),
            pltpu.VMEM((4, 16, 8, 8, 128), f32),
            pltpu.VMEM((16, 128), f32),
            pltpu.SMEM((128,), jnp.int32),
            pltpu.SMEM((384,), f32),
            pltpu.SMEM((128,), jnp.int32),
            dma((4, 16)),
            dma((4, 16)),
            dma((4, 8)),
            dma((32,)),
            dma((32,)),
            dma((4, 8)),
            dma((4, 16)),
            dma((4, 16)),
            dma((2, 4)),
            dma((2, 4)),
            dma((2, 4, 8)),
            dma((4, 8)),
            dma,
            pltpu.VMEM((4, 16, 8, 8, 128), f32),
            pltpu.VMEM((24, 128, 256), f32),
            pltpu.VMEM((16, 8, 32, 128), f32),
        ],
        compiler_params=pltpu.CompilerParams(
            collective_id=0, has_side_effects=True, vmem_limit_bytes=32 * 2**20
        ),
    )(levels, values)


def local_call(kernel, levels, values, out_shape):
    return pl.pallas_call(
        kernel,
        out_shape=jax.ShapeDtypeStruct(out_shape, jnp.float32),
        in_specs=[
            pl.BlockSpec(memory_space=pltpu.SMEM),
            pl.BlockSpec(memory_space=pltpu.VMEM),
        ],
        out_specs=pl.BlockSpec(memory_space=pltpu.VMEM),
        scratch_shapes=[pltpu.VMEM((16, 128, 256), jnp.float32)],
        compiler_params=pltpu.CompilerParams(vmem_limit_bytes=32 * 2**20),
    )(levels, values)


def per_device(grids, levels):
    turned = levels.T
    received = exchange(turned, grids.reshape(128, 4096))
    combined = local_call(backward_kernel, turned, received, (128, 4096))
    return combined.reshape(grids.shape)


def solution(mesh):
    return jax.shard_map(
        per_device,
        mesh=mesh,
        in_specs=(P(("half", "grid"), "dom", None, None), P()),
        out_specs=P(("half", "grid"), "dom", None, None),
        check_vma=False,
    )
```

```python
import jax
import jax.numpy as jnp
from jax import lax
from jax.experimental import pallas as pl
from jax.experimental.pallas import tpu as pltpu
from jax.sharding import PartitionSpec as P

LEV1 = 6
LEV2 = 6
LEV3 = 6
LEV4 = 6
MESH = pl.DeviceIdType.MESH
LOWEST = (LEV1 - 2, LEV2 - 1, LEV3 - 1, LEV4 - 1)


def down_entry(high, h, e, p):
    low = jnp.where(p == e * (1 + high), 1.0, 0.0)
    fine = jnp.where(p == 2 * e + 1, 1.0, 0.0)
    fine = fine - jnp.where((p == 2 * e) | (p == ((2 * e + 2) & 63)), 0.5, 0.0)
    return jnp.where(h == 0, low, fine * high.astype(jnp.float32))


def up_entry(high, h, e, p):
    middle = jnp.where((p == 2 * e + 1) | (p == ((2 * e + 63) & 63)), 0.5, 0.0)
    low = jnp.where(p == e * (1 + high), 1.0, 0.0) + middle * high.astype(jnp.float32)
    fine = jnp.where(p == 2 * e + 1, 1.0, 0.0) * high.astype(jnp.float32)
    return jnp.where(h == 0, low, fine)


def lane_table(entry, high, points_axis):
    point = lax.broadcasted_iota(jnp.int32, (256, 256), points_axis)
    place = lax.broadcasted_iota(jnp.int32, (256, 256), 1 - points_axis)
    value = entry(high, place >> 7, place & 31, point & 63)
    return jnp.where((point >> 6) == ((place >> 5) & 3), value, 0.0).astype(jnp.bfloat16)


def row_table(entry, high, points_axis):
    point = lax.broadcasted_iota(jnp.int32, (128, 128), points_axis)
    place = lax.broadcasted_iota(jnp.int32, (128, 128), 1 - points_axis)
    part = (place >> 3) * 4 + (place & 3)
    value = entry(high, part >> 5, part & 31, point & 63)
    return jnp.where((point >> 6) == ((place >> 2) & 1), value, 0.0).astype(jnp.bfloat16)


def split(values):
    high = values.astype(jnp.bfloat16)
    low = (values - high.astype(jnp.float32)).astype(jnp.bfloat16)
    return high, low


def dot(left, right):
    return jnp.dot(left, right, preferred_element_type=jnp.float32)


def roll_lanes(values):
    return jnp.concatenate(
        [pltpu.roll(values[:, :128], 96, 1), pltpu.roll(values[:, 128:], 96, 1)], axis=1
    )


def swap_halves(first, second):
    front = lax.broadcasted_iota(jnp.int32, first.shape, 1) < 64
    return (
        jnp.where(front, first, pltpu.roll(second, 64, 1)),
        jnp.where(front, pltpu.roll(first, 64, 1), second),
    )


def lanes_product(even, odd, table):
    even_high, even_low = split(even)
    odd_high, odd_low = split(odd)
    out = dot(jnp.concatenate([even_high, even_low, odd_high, odd_low], axis=0), table)
    return out[:128] + out[128:256], out[256:384] + out[384:]


def rows_product(table, values):
    high, low = split(values)
    return dot(table, high) + dot(table, low)


def offsets_of(levels_ref, grid):
    return [levels_ref[axis, grid] - LOWEST[axis] for axis in range(4)]


def cover_of(offsets, b, c, d):
    _, second, third, fourth = offsets
    covered = (1 - b + b * second) * (1 - c + c * third) * (1 - d + d * fourth)
    return covered, covered * ((b * (1 + third) + c) * (1 + fourth) + d)


def own_grid():
    return lax.axis_index("half") * 8 + lax.axis_index("grid")


def blocks_of(offsets, slot):
    _, second, third, fourth = offsets
    d_at = (slot % 2) * fourth
    rest = slot + fourth * (slot // 2 - slot)
    c_at = (rest % 2) * third
    rest = rest + third * (rest // 2 - rest)
    return jnp.where(rest <= second, rest * 4 + c_at * 2 + d_at, 0)


def lower(offsets, x_ref, held, blocks_ref):
    _, b_high, c_high, d_high = offsets
    lane = lane_table(down_entry, d_high, 0)
    row = row_table(down_entry, b_high, 1)
    fine = c_high == 1

    def tile(i, j):
        t = i + 8 * j
        u = i % 4 + 4 * j
        return jnp.where(
            fine, x_ref[:, t * 128 : t * 128 + 128], x_ref[:, u * 128 : u * 128 + 128]
        )

    for i in range(8):
        even01, odd01 = swap_halves(tile(i, 0), tile(i, 1))
        even23, odd23 = swap_halves(tile(i, 2), tile(i, 3))
        held[i], held[8 + i] = lanes_product(
            jnp.concatenate([even01, even23], axis=1),
            jnp.concatenate([odd01, odd23], axis=1),
            lane,
        )
    for m in range(7, -1, -1):
        held[16 + m] = jnp.where(fine, held[m], held[m // 2 + 8 * (m % 2)])
    for m in range(8):
        after = held[17 + m] if m < 7 else roll_lanes(held[16])
        held[8 + m] = held[8 + m] - 0.5 * (held[16 + m] + after)
    for c in range(2):
        for m in range(8):
            out = rows_product(row, held[16 - 8 * c + m])
            for b in range(2):
                for d in range(2):
                    for half in range(2):
                        start = b * 64 + half * 32
                        blocks_ref[half * 8 + m, b * 4 + c * 2 + d] = out[
                            start : start + 32, d * 128 : d * 128 + 128
                        ]


def backward_kernel(levels_ref, recv_ref, out_ref, held):
    offsets = offsets_of(levels_ref, own_grid())
    first, b_high, c_high, d_high = offsets
    inside = lax.axis_index("dom") < lax.shift_left(8, first)

    @pl.when(jnp.logical_not(inside))
    def _():
        out_ref[...] = jnp.zeros_like(out_ref)

    @pl.when(inside)
    def _():
        lane = lane_table(up_entry, d_high, 1)
        row = row_table(up_entry, b_high, 0)

        def rows(c, m):
            columns = []
            for d in range(2):
                parts = []
                for b in range(2):
                    covered, slot = cover_of(offsets, b, c, d)
                    for half in range(2):
                        for group in range(4):
                            part = recv_ref[group, half * 8 + m, slot]
                            parts.append(jnp.where(covered == 1, part, 0.0))
                columns.append(jnp.concatenate(parts, axis=0))
            held[c * 8 + m] = rows_product(row, jnp.concatenate(columns, axis=1))

        def step(i, count, even, odd):
            even, odd = lanes_product(even, odd, lane)
            tiles = swap_halves(even[:, :128], odd[:, :128]) + swap_halves(
                even[:, 128:], odd[:, 128:]
            )
            for j in range(4):
                t = i + j * count
                out_ref[:, t * 128 : t * 128 + 128] = tiles[j]

        for m in range(8):
            rows(0, m)

        @pl.when(c_high == 1)
        def _():
            for m in range(8):
                rows(1, m)
            for m in range(8):
                after = held[m + 1] if m < 7 else roll_lanes(held[0])
                step(m, 8, held[m], held[8 + m] + 0.5 * (held[m] + after))

        @pl.when(c_high == 0)
        def _():
            for i in range(4):
                step(i, 4, held[2 * i], held[2 * i + 1])
            out_ref[:, 2048:] = jnp.zeros((128, 2048), jnp.float32)


def weigh(levels_ref, weight_ref):
    guard = 0x8888
    packed = []
    for grid in range(16):
        first, second, third, fourth = offsets_of(levels_ref, grid)
        packed.append(first + 16 * second + 256 * third + 4096 * fourth)
    rows = lax.broadcasted_iota(jnp.int32, (16, 128), 0)
    corner = lax.broadcasted_iota(jnp.int32, (16, 128), 1)
    bits = [lax.shift_right_logical(corner, place) & 1 for place in range(4)]
    raised = bits[0] + 16 * bits[1] + 256 * bits[2] + 4096 * bits[3]
    for grid in range(16):
        raised = raised + jnp.where(rows == grid, packed[grid], 0)
    count = jnp.zeros((16, 128), jnp.int32)
    for grid in range(16):
        above = ((packed[grid] + guard) - raised) & guard
        count = count + jnp.where(above == guard, 1, 0)
    parity = 1 - 2 * ((bits[0] + bits[1] + bits[2] + bits[3]) & 1)
    signed = jnp.where((count > 0) & (corner < 16), parity, 0).astype(jnp.float32)
    total = jnp.sum(signed, axis=1, keepdims=True)
    weight_ref[...] = jnp.broadcast_to(total, (16, 128))


def exchange_kernel(levels_ref, x_ref, out_ref, *scratch):
    (
        r1,
        acc,
        r3,
        relayed,
        r2,
        o2,
        s2,
        weight_ref,
        slot_ref,
        coef_ref,
        pick_ref,
        send1,
        recv1,
        send2,
        recv2,
        send3,
        recv3,
        send4,
        recv4,
        sendr,
        recvr,
        sendf,
        recvf,
        own,
        send_ref,
        held,
        blocks_ref,
        here,
    ) = [scratch[4 * i : 4 * i + 4] for i in range(4)] + list(scratch[16:])
    half = lax.axis_index("half")
    line = lax.axis_index("grid")
    me = half * 8 + line
    dom = lax.axis_index("dom")
    far = dom // 16
    mine = dom % 4
    my_e = dom // 4

    for s in range(8):
        r2[s, 2] = jnp.zeros((8, 128), jnp.float32)

    barrier = pltpu.get_barrier_semaphore()

    def greet_group(k, _):
        peer = (me + k) % 16
        pl.semaphore_signal(
            barrier, inc=1, device_id={"half": peer // 8, "grid": peer % 8}, device_id_type=MESH
        )
        return 0

    def greet_near(k, _):
        pl.semaphore_signal(
            barrier, inc=1, device_id={"dom": (dom + k) % 32}, device_id_type=MESH
        )
        return 0

    def greet_far(k, _):
        pl.semaphore_signal(
            barrier, inc=1, device_id={"dom": 16 + (dom + k) % 16}, device_id_type=MESH
        )
        return 0

    def answer(k, _):
        pl.semaphore_signal(
            here, inc=1, device_id={"dom": (dom + k) % 16}, device_id_type=MESH
        )
        return 0

    lax.fori_loop(1, 16, greet_group, 0)

    @pl.when(far == 0)
    def _():
        lax.fori_loop(1, 32, greet_near, 0)

    @pl.when(far == 1)
    def _():
        lax.fori_loop(1, 16, greet_far, 0)

    offsets = offsets_of(levels_ref, me)
    lower(offsets, x_ref, held, blocks_ref)
    places = [blocks_of(offsets, slot) for slot in range(8)]

    def pack(c):
        def one(target, _):
            for slot in range(8):
                send_ref[c, target, slot] = blocks_ref[target, places[slot], pl.ds(8 * c, 8), :]
            return 0

        lax.fori_loop(0, 16, one, 0)

    pack(0)

    @pl.when(far == 0)
    def _():
        pl.semaphore_wait(barrier, 30)

    @pl.when(far == 1)
    def _():
        pl.semaphore_wait(barrier, 46)
        lax.fori_loop(0, 16, answer, 0)


    def sized(key, act):
        for option in range(3):

            @pl.when(key == option)
            def _():
                act(8 >> option)

    def copy1(c, source, peer, count):
        return pltpu.make_async_remote_copy(
            src_ref=send_ref.at[c, peer, pl.ds(0, count)],
            dst_ref=r1[c].at[source, pl.ds(0, count)],
            send_sem=send1.at[c, peer],
            recv_sem=recv1.at[c, source],
            device_id={"half": peer // 8, "grid": peer % 8},
            device_id_type=MESH,
        )

    def shared(source, owner_at, act):
        key = source // 8 + far
        direct = (owner_at // 8 == 0) | (source % 8 == owner_at % 8)

        @pl.when((key == 0) & direct)
        def _():
            act(8)

        @pl.when(((key == 0) & jnp.logical_not(direct)) | (key == 1))
        def _():
            act(4)

        @pl.when(key == 2)
        def _():
            act(2)

    def relay(c):
        return pltpu.make_async_remote_copy(
            src_ref=send_ref.at[c, pl.ds(8, 8), pl.ds(4, 4)],
            dst_ref=relayed[c],
            send_sem=sendr.at[c],
            recv_sem=recvr.at[c],
            device_id={"half": 1 - half},
            device_id_type=MESH,
        )

    def forward(c, source, to):
        return pltpu.make_async_remote_copy(
            src_ref=relayed[c].at[to],
            dst_ref=r1[c].at[source, pl.ds(4, 4)],
            send_sem=sendf.at[c, to],
            recv_sem=recvf.at[c, source],
            device_id={"grid": to},
            device_id_type=MESH,
        )

    gives = half + far == 0
    takes = (half == 1) & (far == 0)

    def pass_on(c):
        @pl.when(takes)
        def _():
            relay(c).wait_recv()

            def one(k, _):
                forward(c, line, (line + k) % 8).start()
                return 0

            lax.fori_loop(1, 8, one, 0)

    def start1(c):
        def one(k, _):
            peer = (me + k) % 16
            shared(me, peer, lambda count: copy1(c, me, peer, count).start())
            return 0

        lax.fori_loop(1, 16, one, 0)

    def send(c):
        @pl.when(gives)
        def _():
            relay(c).start()

        start1(c)

    send(0)
    pack(1)
    send(1)
    pack(2)
    pack(3)

    @pl.when(gives)
    def _():
        for c in range(2, 4):
            relay(c).start()

    weigh(levels_ref, weight_ref)
    near = 1 - far
    nearest = jnp.where(dom < 8, 1, 0)

    def table(i, _):
        grid = i // 8
        place = i % 8
        offsets = offsets_of(levels_ref, grid)
        first = offsets[0]
        covered, slot = cover_of(offsets, place // 4, place // 2 % 2, place % 2)
        is_two = jnp.where(first == 2, 1, 0)
        is_one = jnp.where(first == 1, 1, 0) * near
        is_zero = jnp.where(first == 0, 1, 0) * nearest
        slot_ref[i] = slot * (is_two + is_one + is_zero)
        coef_ref[3 * i] = (covered * is_two).astype(jnp.float32)
        coef_ref[3 * i + 1] = (covered * is_one).astype(jnp.float32)
        coef_ref[3 * i + 2] = (covered * is_zero).astype(jnp.float32)
        chosen = blocks_of(offsets, place)
        pick_ref[i] = chosen * 3 + is_one + 2 * is_zero
        return 0

    lax.fori_loop(0, 128, table, 0)

    def tiered(key, act):
        for option in range(3):

            @pl.when(key == option)
            def _():
                act(1 + option)

    def tiers(low, high):
        return (1 - low // 16) + jnp.where((low // 8) + (high // 4) == 0, 1, 0)

    def owner(c, e):
        return 4 * e + c

    def copy2(c, source, e, count):
        return pltpu.make_async_remote_copy(
            src_ref=acc[c].at[e, pl.ds(0, count)],
            dst_ref=r2.at[source, pl.ds(0, count)],
            send_sem=send2.at[c, e],
            recv_sem=recv2.at[source],
            device_id={"dom": owner(c, e)},
            device_id_type=MESH,
        )

    def copy3(c, e, peer, count):
        return pltpu.make_async_remote_copy(
            src_ref=o2.at[peer, pl.ds(0, count)],
            dst_ref=r3[c].at[pl.ds(e * 3, count)],
            send_sem=send3.at[peer],
            recv_sem=recv3.at[c, e],
            device_id={"dom": peer},
            device_id_type=MESH,
        )

    def copy4(c, source, peer, count):
        return pltpu.make_async_remote_copy(
            src_ref=s2.at[c, peer, pl.ds(0, count)],
            dst_ref=out_ref.at[c, source, pl.ds(0, count)],
            send_sem=send4.at[c, peer],
            recv_sem=recv4.at[c, source],
            device_id={"half": peer // 8, "grid": peer % 8},
            device_id_type=MESH,
        )

    def part(ref, kind, p):
        return ref[p // 2, kind, (p % 2) * 4 : (p % 2) * 4 + 4, :]

    def put(ref, kind, p, value):
        ref[p // 2, kind, (p % 2) * 4 : (p % 2) * 4 + 4, :] = value

    def joined(p):
        p = p % 32
        return part(r2, 0, 2 * p) + part(r2, 1, p)

    def coarse(q):
        q = q % 16
        return joined(2 * q) + part(r2, 2, q)

    def lift():
        for q in range(16):
            here = coarse(q)
            after = coarse(q + 1)
            middle = joined(2 * q + 1) - 0.5 * (joined(2 * q) + joined(2 * q + 2))
            put(o2, 2, q, here)
            put(o2, 1, 2 * q, here)
            put(o2, 1, 2 * q + 1, middle + 0.5 * (here + after))
        for s in range(32):
            here = part(o2, 1, s)
            after = part(o2, 1, (s + 1) % 32)
            fine = part(r2, 0, 2 * s + 1) - 0.5 * (
                part(r2, 0, 2 * s) + part(r2, 0, (2 * s + 2) % 64)
            )
            put(o2, 0, 2 * s, here)
            put(o2, 0, 2 * s + 1, fine + 0.5 * (here + after))

    def arrive(c):
        def wait1(k, _):
            source = (me + 16 - k) % 16
            shared(source, me, lambda count: copy1(c, source, source, count).wait_recv())

            @pl.when((source // 8 == 0) & takes & (source % 8 != line))
            def _():
                forward(c, source % 8, source % 8).wait_recv()

            return 0

        lax.fori_loop(1, 16, wait1, 0)

    def summed(c):
        def keep(slot, _):
            r1[c][me, slot] = send_ref[c, me, slot]
            return 0

        lax.fori_loop(0, 8, keep, 0)

        def add(block, _):
            sums = [jnp.zeros((8, 128), jnp.float32) for _ in range(2)]
            for source in range(16):
                at = source * 8 + block
                value = r1[c][source, slot_ref[at]] * weight_ref[pl.ds(source, 1), :]
                for kind in range(2):
                    sums[kind] = sums[kind] + value * coef_ref[3 * at + kind]
            for kind in range(2):
                acc[c][block, kind] = sums[kind]
            return 0

        lax.fori_loop(0, 8, add, 0)
        total = jnp.zeros((8, 128), jnp.float32)
        for source in range(16):
            value = r1[c][source, 0] * weight_ref[pl.ds(source, 1), :]
            total = total + value * coef_ref[3 * source * 8 + 2]
        acc[c][0, 2] = total

        def start2(k, _):
            e = (my_e + k) % 8
            peer = owner(c, e)

            @pl.when(peer != dom)
            def _():
                tiered(tiers(dom, peer), lambda count: copy2(c, dom, e, count).start())

            return 0

        lax.fori_loop(0, 8, start2, 0)

    def owned(c):
        @pl.when(mine == c)
        def _():
            for kind in range(2):
                r2[dom, kind] = acc[c][my_e, kind]

            @pl.when(my_e == 0)
            def _():
                r2[dom, 2] = acc[c][my_e, 2]

            def wait2(k, _):
                source = (dom + 32 - k) % 32
                tiered(
                    tiers(source, dom), lambda count: copy2(c, source, my_e, count).wait_recv()
                )
                return 0

            lax.fori_loop(1, 32, wait2, 0)
            lift()

            def start3(k, _):
                peer = (dom + k) % 32
                tiered(tiers(peer, dom), lambda count: copy3(c, my_e, peer, count).start())
                return 0

            lax.fori_loop(1, 32, start3, 0)
            r3[c][my_e * 3] = o2[dom, 0]

            @pl.when(far == 0)
            def _():
                r3[c][my_e * 3 + 1] = o2[dom, 1]

            @pl.when(my_e == 0)
            def _():
                r3[c][my_e * 3 + 2] = o2[dom, 2]

    def deliver(c):
        def wait3(k, _):
            e = (my_e + 8 - k) % 8
            peer = owner(c, e)

            @pl.when(peer != dom)
            def _():
                tiered(tiers(dom, peer), lambda count: copy3(c, e, dom, count).wait_recv())

            return 0

        lax.fori_loop(0, 8, wait3, 0)

        def fill(peer):
            for slot in range(8):
                s2[c, peer, slot] = r3[c][pick_ref[peer * 8 + slot]]

        def start4(k, _):
            peer = (me + k) % 16
            fill(peer)
            sized(peer // 8 + far, lambda count: copy4(c, me, peer, count).start())
            return 0

        lax.fori_loop(1, 16, start4, 0)
        fill(me)

    pass_on(0)
    start1(2)
    pass_on(1)
    arrive(0)
    start1(3)

    @pl.when(far == 0)
    def _():
        pl.semaphore_wait(here, 16)

    summed(0)
    pass_on(2)
    owned(0)
    pass_on(3)
    arrive(1)
    summed(1)
    owned(1)
    arrive(2)
    summed(2)
    deliver(0)
    owned(2)
    deliver(1)
    arrive(3)
    summed(3)
    owned(3)
    deliver(2)
    deliver(3)
    home = pltpu.make_async_copy(s2.at[:, me], out_ref.at[:, me], own)
    home.start()

    for c in range(4):

        def wait4(k, _):
            source = (me + 16 - k) % 16
            sized(half + far, lambda count: copy4(c, source, source, count).wait_recv())
            return 0

        lax.fori_loop(1, 16, wait4, 0)

    home.wait()

    def sent_group(k, _):
        peer = (me + k) % 16
        for c in range(4):
            shared(me, peer, lambda count: copy1(c, me, peer, count).wait_send())
            sized(peer // 8 + far, lambda count: copy4(c, me, peer, count).wait_send())
        return 0

    lax.fori_loop(1, 16, sent_group, 0)

    @pl.when(gives)
    def _():
        for c in range(4):
            relay(c).wait_send()

    @pl.when(takes)
    def _():
        def passed(k, _):
            for c in range(4):
                forward(c, line, (line + k) % 8).wait_send()
            return 0

        lax.fori_loop(1, 8, passed, 0)

    for c in range(4):

        def sent2(e, _):
            peer = owner(c, e)

            @pl.when(peer != dom)
            def _():
                tiered(tiers(dom, peer), lambda count: copy2(c, dom, e, count).wait_send())

            return 0

        lax.fori_loop(0, 8, sent2, 0)

    def sent3(k, _):
        peer = (dom + k) % 32
        tiered(tiers(peer, dom), lambda count: copy3(0, my_e, peer, count).wait_send())
        return 0

    lax.fori_loop(1, 32, sent3, 0)


def exchange(levels, values):
    dma = pltpu.SemaphoreType.DMA
    f32 = jnp.float32
    return pl.pallas_call(
        exchange_kernel,
        out_shape=jax.ShapeDtypeStruct((4, 16, 8, 8, 128), f32),
        in_specs=[
            pl.BlockSpec(memory_space=pltpu.SMEM),
            pl.BlockSpec(memory_space=pltpu.VMEM),
        ],
        out_specs=pl.BlockSpec(memory_space=pl.ANY),
        scratch_shapes=[pltpu.VMEM((16, 8, 8, 128), f32)] * 4
        + [pltpu.VMEM((8, 3, 8, 128), f32)] * 4
        + [pltpu.VMEM((24, 8, 128), f32)] * 4
        + [pltpu.VMEM((8, 4, 8, 128), f32)] * 4
        + [
            pltpu.VMEM((32, 3, 8, 128), f32),
            pltpu.VMEM((32, 3, 8, 128), f32),
            pltpu.VMEM((4, 16, 8, 8, 128), f32),
            pltpu.VMEM((16, 128), f32),
            pltpu.SMEM((128,), jnp.int32),
            pltpu.SMEM((384,), f32),
            pltpu.SMEM((128,), jnp.int32),
            dma((4, 16)),
            dma((4, 16)),
            dma((4, 8)),
            dma((32,)),
            dma((32,)),
            dma((4, 8)),
            dma((4, 16)),
            dma((4, 16)),
            dma((4,)),
            dma((4,)),
            dma((4, 8)),
            dma((4, 8)),
            dma,
            pltpu.VMEM((4, 16, 8, 8, 128), f32),
            pltpu.VMEM((24, 128, 256), f32),
            pltpu.VMEM((16, 8, 32, 128), f32),
            pltpu.SemaphoreType.REGULAR,
        ],
        compiler_params=pltpu.CompilerParams(
            collective_id=0, has_side_effects=True, vmem_limit_bytes=32 * 2**20
        ),
    )(levels, values)


def local_call(kernel, levels, values, out_shape):
    return pl.pallas_call(
        kernel,
        out_shape=jax.ShapeDtypeStruct(out_shape, jnp.float32),
        in_specs=[
            pl.BlockSpec(memory_space=pltpu.SMEM),
            pl.BlockSpec(memory_space=pltpu.VMEM),
        ],
        out_specs=pl.BlockSpec(memory_space=pltpu.VMEM),
        scratch_shapes=[pltpu.VMEM((16, 128, 256), jnp.float32)],
        compiler_params=pltpu.CompilerParams(vmem_limit_bytes=32 * 2**20),
    )(levels, values)


def per_device(grids, levels):
    turned = levels.T
    received = exchange(turned, grids.reshape(128, 4096))
    combined = local_call(backward_kernel, turned, received, (128, 4096))
    return combined.reshape(grids.shape)


def solution(mesh):
    return jax.shard_map(
        per_device,
        mesh=mesh,
        in_specs=(P(("half", "grid"), "dom", None, None), P()),
        out_specs=P(("half", "grid"), "dom", None, None),
        check_vma=False,
    )
```

```python
import jax
import jax.numpy as jnp
from jax import lax
from jax.experimental import pallas as pl
from jax.experimental.pallas import tpu as pltpu
from jax.sharding import PartitionSpec as P

LEV1 = 6
LEV2 = 6
LEV3 = 6
LEV4 = 6
MESH = pl.DeviceIdType.MESH
LOWEST = (LEV1 - 2, LEV2 - 1, LEV3 - 1, LEV4 - 1)


def down_entry(high, h, e, p):
    low = jnp.where(p == e * (1 + high), 1.0, 0.0)
    fine = jnp.where(p == 2 * e + 1, 1.0, 0.0)
    fine = fine - jnp.where((p == 2 * e) | (p == ((2 * e + 2) & 63)), 0.5, 0.0)
    return jnp.where(h == 0, low, fine * high.astype(jnp.float32))


def up_entry(high, h, e, p):
    middle = jnp.where((p == 2 * e + 1) | (p == ((2 * e + 63) & 63)), 0.5, 0.0)
    low = jnp.where(p == e * (1 + high), 1.0, 0.0) + middle * high.astype(jnp.float32)
    fine = jnp.where(p == 2 * e + 1, 1.0, 0.0) * high.astype(jnp.float32)
    return jnp.where(h == 0, low, fine)


def lane_table(entry, high, points_axis):
    point = lax.broadcasted_iota(jnp.int32, (256, 256), points_axis)
    place = lax.broadcasted_iota(jnp.int32, (256, 256), 1 - points_axis)
    value = entry(high, place >> 7, place & 31, point & 63)
    return jnp.where((point >> 6) == ((place >> 5) & 3), value, 0.0).astype(jnp.bfloat16)


def row_table(entry, high, points_axis):
    point = lax.broadcasted_iota(jnp.int32, (128, 128), points_axis)
    place = lax.broadcasted_iota(jnp.int32, (128, 128), 1 - points_axis)
    part = (place >> 3) * 4 + (place & 3)
    value = entry(high, part >> 5, part & 31, point & 63)
    return jnp.where((point >> 6) == ((place >> 2) & 1), value, 0.0).astype(jnp.bfloat16)


def split(values):
    high = values.astype(jnp.bfloat16)
    low = (values - high.astype(jnp.float32)).astype(jnp.bfloat16)
    return high, low


def dot(left, right):
    return jnp.dot(left, right, preferred_element_type=jnp.float32)


def roll_lanes(values):
    return jnp.concatenate(
        [pltpu.roll(values[:, :128], 96, 1), pltpu.roll(values[:, 128:], 96, 1)], axis=1
    )


def swap_halves(first, second):
    front = lax.broadcasted_iota(jnp.int32, first.shape, 1) < 64
    return (
        jnp.where(front, first, pltpu.roll(second, 64, 1)),
        jnp.where(front, pltpu.roll(first, 64, 1), second),
    )


def lanes_product(even, odd, table):
    even_high, even_low = split(even)
    odd_high, odd_low = split(odd)
    out = dot(jnp.concatenate([even_high, even_low, odd_high, odd_low], axis=0), table)
    return out[:128] + out[128:256], out[256:384] + out[384:]


def rows_product(table, values):
    high, low = split(values)
    return dot(table, high) + dot(table, low)


def offsets_of(levels_ref, grid):
    return [levels_ref[axis, grid] - LOWEST[axis] for axis in range(4)]


def cover_of(offsets, b, c, d):
    _, second, third, fourth = offsets
    covered = (1 - b + b * second) * (1 - c + c * third) * (1 - d + d * fourth)
    return covered, covered * ((b * (1 + third) + c) * (1 + fourth) + d)


def own_grid():
    return lax.axis_index("half") * 8 + lax.axis_index("grid")


def blocks_of(offsets, slot):
    _, second, third, fourth = offsets
    d_at = (slot % 2) * fourth
    rest = slot + fourth * (slot // 2 - slot)
    c_at = (rest % 2) * third
    rest = rest + third * (rest // 2 - rest)
    return jnp.where(rest <= second, rest * 4 + c_at * 2 + d_at, 0)


def lower(offsets, x_ref, held, blocks_ref):
    _, b_high, c_high, d_high = offsets
    lane = lane_table(down_entry, d_high, 0)
    row = row_table(down_entry, b_high, 1)
    fine = c_high == 1

    def tile(i, j):
        t = i + 8 * j
        u = i % 4 + 4 * j
        return jnp.where(
            fine, x_ref[:, t * 128 : t * 128 + 128], x_ref[:, u * 128 : u * 128 + 128]
        )

    for i in range(8):
        even01, odd01 = swap_halves(tile(i, 0), tile(i, 1))
        even23, odd23 = swap_halves(tile(i, 2), tile(i, 3))
        held[i], held[8 + i] = lanes_product(
            jnp.concatenate([even01, even23], axis=1),
            jnp.concatenate([odd01, odd23], axis=1),
            lane,
        )
    for m in range(7, -1, -1):
        held[16 + m] = jnp.where(fine, held[m], held[m // 2 + 8 * (m % 2)])
    for m in range(8):
        after = held[17 + m] if m < 7 else roll_lanes(held[16])
        held[8 + m] = held[8 + m] - 0.5 * (held[16 + m] + after)
    for c in range(2):
        for m in range(8):
            out = rows_product(row, held[16 - 8 * c + m])
            for b in range(2):
                for d in range(2):
                    for half in range(2):
                        start = b * 64 + half * 32
                        blocks_ref[half * 8 + m, b * 4 + c * 2 + d] = out[
                            start : start + 32, d * 128 : d * 128 + 128
                        ]


def backward_kernel(levels_ref, recv_ref, out_ref, held):
    offsets = offsets_of(levels_ref, own_grid())
    first, b_high, c_high, d_high = offsets
    inside = lax.axis_index("dom") < lax.shift_left(8, first)

    @pl.when(jnp.logical_not(inside))
    def _():
        out_ref[...] = jnp.zeros_like(out_ref)

    @pl.when(inside)
    def _():
        lane = lane_table(up_entry, d_high, 1)
        row = row_table(up_entry, b_high, 0)

        def rows(c, m):
            columns = []
            for d in range(2):
                parts = []
                for b in range(2):
                    covered, slot = cover_of(offsets, b, c, d)
                    for half in range(2):
                        for group in range(4):
                            part = recv_ref[group, half * 8 + m, slot]
                            parts.append(jnp.where(covered == 1, part, 0.0))
                columns.append(jnp.concatenate(parts, axis=0))
            held[c * 8 + m] = rows_product(row, jnp.concatenate(columns, axis=1))

        def step(i, count, even, odd):
            even, odd = lanes_product(even, odd, lane)
            tiles = swap_halves(even[:, :128], odd[:, :128]) + swap_halves(
                even[:, 128:], odd[:, 128:]
            )
            for j in range(4):
                t = i + j * count
                out_ref[:, t * 128 : t * 128 + 128] = tiles[j]

        for m in range(8):
            rows(0, m)

        @pl.when(c_high == 1)
        def _():
            for m in range(8):
                rows(1, m)
            for m in range(8):
                after = held[m + 1] if m < 7 else roll_lanes(held[0])
                step(m, 8, held[m], held[8 + m] + 0.5 * (held[m] + after))

        @pl.when(c_high == 0)
        def _():
            for i in range(4):
                step(i, 4, held[2 * i], held[2 * i + 1])
            out_ref[:, 2048:] = jnp.zeros((128, 2048), jnp.float32)


def weigh(levels_ref, weight_ref):
    guard = 0x8888
    packed = []
    for grid in range(16):
        first, second, third, fourth = offsets_of(levels_ref, grid)
        packed.append(first + 16 * second + 256 * third + 4096 * fourth)
    rows = lax.broadcasted_iota(jnp.int32, (16, 128), 0)
    corner = lax.broadcasted_iota(jnp.int32, (16, 128), 1)
    bits = [lax.shift_right_logical(corner, place) & 1 for place in range(4)]
    raised = bits[0] + 16 * bits[1] + 256 * bits[2] + 4096 * bits[3]
    for grid in range(16):
        raised = raised + jnp.where(rows == grid, packed[grid], 0)
    count = jnp.zeros((16, 128), jnp.int32)
    for grid in range(16):
        above = ((packed[grid] + guard) - raised) & guard
        count = count + jnp.where(above == guard, 1, 0)
    parity = 1 - 2 * ((bits[0] + bits[1] + bits[2] + bits[3]) & 1)
    signed = jnp.where((count > 0) & (corner < 16), parity, 0).astype(jnp.float32)
    total = jnp.sum(signed, axis=1, keepdims=True)
    weight_ref[...] = jnp.broadcast_to(total, (16, 128))


def exchange_kernel(levels_ref, x_ref, out_ref, *scratch):
    (
        r1,
        acc,
        r3,
        relayed,
        r2,
        o2,
        s2,
        weight_ref,
        slot_ref,
        coef_ref,
        pick_ref,
        send1,
        recv1,
        send2,
        recv2,
        send3,
        recv3,
        send4,
        recv4,
        sendr,
        recvr,
        sendf,
        recvf,
        own,
        send_ref,
        held,
        blocks_ref,
        here,
    ) = [scratch[4 * i : 4 * i + 4] for i in range(4)] + list(scratch[16:])
    half = lax.axis_index("half")
    line = lax.axis_index("grid")
    me = half * 8 + line
    dom = lax.axis_index("dom")
    far = dom // 16
    mine = dom % 4
    my_e = dom // 4

    for s in range(8):
        r2[s, 2] = jnp.zeros((8, 128), jnp.float32)

    barrier = pltpu.get_barrier_semaphore()

    def greet_group(k, _):
        peer = (me + k) % 16
        pl.semaphore_signal(
            barrier, inc=1, device_id={"half": peer // 8, "grid": peer % 8}, device_id_type=MESH
        )
        return 0

    def greet_near(k, _):
        pl.semaphore_signal(
            barrier, inc=1, device_id={"dom": (dom + k) % 32}, device_id_type=MESH
        )
        return 0

    def greet_far(k, _):
        pl.semaphore_signal(
            barrier, inc=1, device_id={"dom": 16 + (dom + k) % 16}, device_id_type=MESH
        )
        return 0

    def answer(k, _):
        pl.semaphore_signal(
            here, inc=1, device_id={"dom": (dom + k) % 16}, device_id_type=MESH
        )
        return 0

    lax.fori_loop(1, 16, greet_group, 0)

    @pl.when(far == 0)
    def _():
        lax.fori_loop(1, 32, greet_near, 0)

    @pl.when(far == 1)
    def _():
        lax.fori_loop(1, 16, greet_far, 0)

    offsets = offsets_of(levels_ref, me)
    lower(offsets, x_ref, held, blocks_ref)
    places = [blocks_of(offsets, slot) for slot in range(8)]

    def pack(c):
        def one(target, _):
            for slot in range(8):
                send_ref[c, target, slot] = blocks_ref[target, places[slot], pl.ds(8 * c, 8), :]
            return 0

        lax.fori_loop(0, 16, one, 0)

    pack(0)

    @pl.when(far == 0)
    def _():
        pl.semaphore_wait(barrier, 30)

    @pl.when(far == 1)
    def _():
        pl.semaphore_wait(barrier, 46)
        lax.fori_loop(0, 16, answer, 0)


    def sized(key, act):
        for option in range(3):

            @pl.when(key == option)
            def _():
                act(8 >> option)

    def copy1(c, source, peer, count):
        return pltpu.make_async_remote_copy(
            src_ref=send_ref.at[c, peer, pl.ds(0, count)],
            dst_ref=r1[c].at[source, pl.ds(0, count)],
            send_sem=send1.at[c, peer],
            recv_sem=recv1.at[c, source],
            device_id={"half": peer // 8, "grid": peer % 8},
            device_id_type=MESH,
        )

    def shared(source, owner_at, act):
        key = source // 8 + far
        direct = (owner_at // 8 == 0) | (source % 8 == owner_at % 8)

        @pl.when((key == 0) & direct)
        def _():
            act(8)

        @pl.when(((key == 0) & jnp.logical_not(direct)) | (key == 1))
        def _():
            act(4)

        @pl.when(key == 2)
        def _():
            act(2)

    def relay(c):
        return pltpu.make_async_remote_copy(
            src_ref=send_ref.at[c, pl.ds(8, 8), pl.ds(4, 4)],
            dst_ref=relayed[c],
            send_sem=sendr.at[c],
            recv_sem=recvr.at[c],
            device_id={"half": 1 - half},
            device_id_type=MESH,
        )

    def forward(c, source, to):
        return pltpu.make_async_remote_copy(
            src_ref=relayed[c].at[to],
            dst_ref=r1[c].at[source, pl.ds(4, 4)],
            send_sem=sendf.at[c, to],
            recv_sem=recvf.at[c, source],
            device_id={"grid": to},
            device_id_type=MESH,
        )

    gives = half + far == 0
    takes = (half == 1) & (far == 0)

    def pass_on(c):
        @pl.when(takes)
        def _():
            relay(c).wait_recv()

            def one(k, _):
                forward(c, line, (line + k) % 8).start()
                return 0

            lax.fori_loop(1, 8, one, 0)

    def ordered(k):
        step = (k - 1) // 2
        away = 4 + step // 2 - (step % 2) * (1 + 2 * (step // 2))
        return (half + k % 2) % 2 * 8 + (line + away) % 8

    def start1(c):
        def one(k, _):
            peer = ordered(k)
            shared(me, peer, lambda count: copy1(c, me, peer, count).start())
            return 0

        lax.fori_loop(1, 16, one, 0)

    def send(c):
        @pl.when(gives)
        def _():
            relay(c).start()

        start1(c)

    send(0)
    pack(1)
    send(1)
    pack(2)
    pack(3)

    @pl.when(gives)
    def _():
        for c in range(2, 4):
            relay(c).start()

    weigh(levels_ref, weight_ref)
    near = 1 - far
    nearest = jnp.where(dom < 8, 1, 0)

    def table(i, _):
        grid = i // 8
        place = i % 8
        offsets = offsets_of(levels_ref, grid)
        first = offsets[0]
        covered, slot = cover_of(offsets, place // 4, place // 2 % 2, place % 2)
        is_two = jnp.where(first == 2, 1, 0)
        is_one = jnp.where(first == 1, 1, 0) * near
        is_zero = jnp.where(first == 0, 1, 0) * nearest
        slot_ref[i] = slot * (is_two + is_one + is_zero)
        coef_ref[3 * i] = (covered * is_two).astype(jnp.float32)
        coef_ref[3 * i + 1] = (covered * is_one).astype(jnp.float32)
        coef_ref[3 * i + 2] = (covered * is_zero).astype(jnp.float32)
        chosen = blocks_of(offsets, place)
        pick_ref[i] = chosen * 3 + is_one + 2 * is_zero
        return 0

    lax.fori_loop(0, 128, table, 0)

    def tiered(key, act):
        for option in range(3):

            @pl.when(key == option)
            def _():
                act(1 + option)

    def tiers(low, high):
        return (1 - low // 16) + jnp.where((low // 8) + (high // 4) == 0, 1, 0)

    def owner(c, e):
        return 4 * e + c

    def copy2(c, source, e, count):
        return pltpu.make_async_remote_copy(
            src_ref=acc[c].at[e, pl.ds(0, count)],
            dst_ref=r2.at[source, pl.ds(0, count)],
            send_sem=send2.at[c, e],
            recv_sem=recv2.at[source],
            device_id={"dom": owner(c, e)},
            device_id_type=MESH,
        )

    def copy3(c, e, peer, count):
        return pltpu.make_async_remote_copy(
            src_ref=o2.at[peer, pl.ds(0, count)],
            dst_ref=r3[c].at[pl.ds(e * 3, count)],
            send_sem=send3.at[peer],
            recv_sem=recv3.at[c, e],
            device_id={"dom": peer},
            device_id_type=MESH,
        )

    def copy4(c, source, peer, count):
        return pltpu.make_async_remote_copy(
            src_ref=s2.at[c, peer, pl.ds(0, count)],
            dst_ref=out_ref.at[c, source, pl.ds(0, count)],
            send_sem=send4.at[c, peer],
            recv_sem=recv4.at[c, source],
            device_id={"half": peer // 8, "grid": peer % 8},
            device_id_type=MESH,
        )

    def part(ref, kind, p):
        return ref[p // 2, kind, (p % 2) * 4 : (p % 2) * 4 + 4, :]

    def put(ref, kind, p, value):
        ref[p // 2, kind, (p % 2) * 4 : (p % 2) * 4 + 4, :] = value

    def joined(p):
        p = p % 32
        return part(r2, 0, 2 * p) + part(r2, 1, p)

    def coarse(q):
        q = q % 16
        return joined(2 * q) + part(r2, 2, q)

    def lift():
        for q in range(16):
            here = coarse(q)
            after = coarse(q + 1)
            middle = joined(2 * q + 1) - 0.5 * (joined(2 * q) + joined(2 * q + 2))
            put(o2, 2, q, here)
            put(o2, 1, 2 * q, here)
            put(o2, 1, 2 * q + 1, middle + 0.5 * (here + after))
        for s in range(32):
            here = part(o2, 1, s)
            after = part(o2, 1, (s + 1) % 32)
            fine = part(r2, 0, 2 * s + 1) - 0.5 * (
                part(r2, 0, 2 * s) + part(r2, 0, (2 * s + 2) % 64)
            )
            put(o2, 0, 2 * s, here)
            put(o2, 0, 2 * s + 1, fine + 0.5 * (here + after))

    def arrive(c):
        def wait1(k, _):
            source = (me + 16 - k) % 16
            shared(source, me, lambda count: copy1(c, source, source, count).wait_recv())

            @pl.when((source // 8 == 0) & takes & (source % 8 != line))
            def _():
                forward(c, source % 8, source % 8).wait_recv()

            return 0

        lax.fori_loop(1, 16, wait1, 0)

    def summed(c):
        def keep(slot, _):
            r1[c][me, slot] = send_ref[c, me, slot]
            return 0

        lax.fori_loop(0, 8, keep, 0)

        def add(block, _):
            sums = [jnp.zeros((8, 128), jnp.float32) for _ in range(2)]
            for source in range(16):
                at = source * 8 + block
                value = r1[c][source, slot_ref[at]] * weight_ref[pl.ds(source, 1), :]
                for kind in range(2):
                    sums[kind] = sums[kind] + value * coef_ref[3 * at + kind]
            for kind in range(2):
                acc[c][block, kind] = sums[kind]
            return 0

        lax.fori_loop(0, 8, add, 0)
        total = jnp.zeros((8, 128), jnp.float32)
        for source in range(16):
            value = r1[c][source, 0] * weight_ref[pl.ds(source, 1), :]
            total = total + value * coef_ref[3 * source * 8 + 2]
        acc[c][0, 2] = total

        def start2(k, _):
            e = (my_e + k) % 8
            peer = owner(c, e)

            @pl.when(peer != dom)
            def _():
                tiered(tiers(dom, peer), lambda count: copy2(c, dom, e, count).start())

            return 0

        lax.fori_loop(0, 8, start2, 0)

    def owned(c):
        @pl.when(mine == c)
        def _():
            for kind in range(2):
                r2[dom, kind] = acc[c][my_e, kind]

            @pl.when(my_e == 0)
            def _():
                r2[dom, 2] = acc[c][my_e, 2]

            def wait2(k, _):
                source = (dom + 32 - k) % 32
                tiered(
                    tiers(source, dom), lambda count: copy2(c, source, my_e, count).wait_recv()
                )
                return 0

            lax.fori_loop(1, 32, wait2, 0)
            lift()

            def start3(k, _):
                peer = (dom + k) % 32
                tiered(tiers(peer, dom), lambda count: copy3(c, my_e, peer, count).start())
                return 0

            lax.fori_loop(1, 32, start3, 0)
            r3[c][my_e * 3] = o2[dom, 0]

            @pl.when(far == 0)
            def _():
                r3[c][my_e * 3 + 1] = o2[dom, 1]

            @pl.when(my_e == 0)
            def _():
                r3[c][my_e * 3 + 2] = o2[dom, 2]

    def deliver(c):
        def wait3(k, _):
            e = (my_e + 8 - k) % 8
            peer = owner(c, e)

            @pl.when(peer != dom)
            def _():
                tiered(tiers(dom, peer), lambda count: copy3(c, e, dom, count).wait_recv())

            return 0

        lax.fori_loop(0, 8, wait3, 0)

        def fill(peer):
            for slot in range(8):
                s2[c, peer, slot] = r3[c][pick_ref[peer * 8 + slot]]

        def start4(k, _):
            peer = ordered(k)
            fill(peer)
            sized(peer // 8 + far, lambda count: copy4(c, me, peer, count).start())
            return 0

        lax.fori_loop(1, 16, start4, 0)
        fill(me)

    pass_on(0)
    start1(2)
    pass_on(1)
    arrive(0)
    start1(3)

    @pl.when(far == 0)
    def _():
        pl.semaphore_wait(here, 16)

    summed(0)
    pass_on(2)
    pass_on(3)
    owned(0)
    arrive(1)
    summed(1)
    deliver(0)
    owned(1)
    arrive(2)
    summed(2)
    deliver(1)
    owned(2)
    arrive(3)
    summed(3)
    deliver(2)
    owned(3)
    deliver(3)

    home = pltpu.make_async_copy(s2.at[:, me], out_ref.at[:, me], own)
    home.start()

    for c in range(4):

        def wait4(k, _):
            source = (me + 16 - k) % 16
            sized(half + far, lambda count: copy4(c, source, source, count).wait_recv())
            return 0

        lax.fori_loop(1, 16, wait4, 0)

    home.wait()

    def sent_group(k, _):
        peer = (me + k) % 16
        for c in range(4):
            shared(me, peer, lambda count: copy1(c, me, peer, count).wait_send())
            sized(peer // 8 + far, lambda count: copy4(c, me, peer, count).wait_send())
        return 0

    lax.fori_loop(1, 16, sent_group, 0)

    @pl.when(gives)
    def _():
        for c in range(4):
            relay(c).wait_send()

    @pl.when(takes)
    def _():
        def passed(k, _):
            for c in range(4):
                forward(c, line, (line + k) % 8).wait_send()
            return 0

        lax.fori_loop(1, 8, passed, 0)

    for c in range(4):

        def sent2(e, _):
            peer = owner(c, e)

            @pl.when(peer != dom)
            def _():
                tiered(tiers(dom, peer), lambda count: copy2(c, dom, e, count).wait_send())

            return 0

        lax.fori_loop(0, 8, sent2, 0)

    def sent3(k, _):
        peer = (dom + k) % 32
        tiered(tiers(peer, dom), lambda count: copy3(0, my_e, peer, count).wait_send())
        return 0

    lax.fori_loop(1, 32, sent3, 0)


def exchange(levels, values):
    dma = pltpu.SemaphoreType.DMA
    f32 = jnp.float32
    return pl.pallas_call(
        exchange_kernel,
        out_shape=jax.ShapeDtypeStruct((4, 16, 8, 8, 128), f32),
        in_specs=[
            pl.BlockSpec(memory_space=pltpu.SMEM),
            pl.BlockSpec(memory_space=pltpu.VMEM),
        ],
        out_specs=pl.BlockSpec(memory_space=pl.ANY),
        scratch_shapes=[pltpu.VMEM((16, 8, 8, 128), f32)] * 4
        + [pltpu.VMEM((8, 3, 8, 128), f32)] * 4
        + [pltpu.VMEM((24, 8, 128), f32)] * 4
        + [pltpu.VMEM((8, 4, 8, 128), f32)] * 4
        + [
            pltpu.VMEM((32, 3, 8, 128), f32),
            pltpu.VMEM((32, 3, 8, 128), f32),
            pltpu.VMEM((4, 16, 8, 8, 128), f32),
            pltpu.VMEM((16, 128), f32),
            pltpu.SMEM((128,), jnp.int32),
            pltpu.SMEM((384,), f32),
            pltpu.SMEM((128,), jnp.int32),
            dma((4, 16)),
            dma((4, 16)),
            dma((4, 8)),
            dma((32,)),
            dma((32,)),
            dma((4, 8)),
            dma((4, 16)),
            dma((4, 16)),
            dma((4,)),
            dma((4,)),
            dma((4, 8)),
            dma((4, 8)),
            dma,
            pltpu.VMEM((4, 16, 8, 8, 128), f32),
            pltpu.VMEM((24, 128, 256), f32),
            pltpu.VMEM((16, 8, 32, 128), f32),
            pltpu.SemaphoreType.REGULAR,
        ],
        compiler_params=pltpu.CompilerParams(
            collective_id=0, has_side_effects=True, vmem_limit_bytes=32 * 2**20
        ),
    )(levels, values)


def local_call(kernel, levels, values, out_shape):
    return pl.pallas_call(
        kernel,
        out_shape=jax.ShapeDtypeStruct(out_shape, jnp.float32),
        in_specs=[
            pl.BlockSpec(memory_space=pltpu.SMEM),
            pl.BlockSpec(memory_space=pltpu.VMEM),
        ],
        out_specs=pl.BlockSpec(memory_space=pltpu.VMEM),
        scratch_shapes=[pltpu.VMEM((16, 128, 256), jnp.float32)],
        compiler_params=pltpu.CompilerParams(vmem_limit_bytes=32 * 2**20),
    )(levels, values)


def per_device(grids, levels):
    turned = levels.T
    received = exchange(turned, grids.reshape(128, 4096))
    combined = local_call(backward_kernel, turned, received, (128, 4096))
    return combined.reshape(grids.shape)


def solution(mesh):
    return jax.shard_map(
        per_device,
        mesh=mesh,
        in_specs=(P(("half", "grid"), "dom", None, None), P()),
        out_specs=P(("half", "grid"), "dom", None, None),
        check_vma=False,
    )
```

```python
import jax
import jax.numpy as jnp
from jax import lax
from jax.experimental import pallas as pl
from jax.experimental.pallas import tpu as pltpu
from jax.sharding import PartitionSpec as P

LEV1 = 6
LEV2 = 6
LEV3 = 6
LEV4 = 6
MESH = pl.DeviceIdType.MESH
LOWEST = (LEV1 - 2, LEV2 - 1, LEV3 - 1, LEV4 - 1)


def down_entry(high, h, e, p):
    low = jnp.where(p == e * (1 + high), 1.0, 0.0)
    fine = jnp.where(p == 2 * e + 1, 1.0, 0.0)
    fine = fine - jnp.where((p == 2 * e) | (p == ((2 * e + 2) & 63)), 0.5, 0.0)
    return jnp.where(h == 0, low, fine * high.astype(jnp.float32))


def up_entry(high, h, e, p):
    middle = jnp.where((p == 2 * e + 1) | (p == ((2 * e + 63) & 63)), 0.5, 0.0)
    low = jnp.where(p == e * (1 + high), 1.0, 0.0) + middle * high.astype(jnp.float32)
    fine = jnp.where(p == 2 * e + 1, 1.0, 0.0) * high.astype(jnp.float32)
    return jnp.where(h == 0, low, fine)


def lane_table(entry, high, points_axis):
    point = lax.broadcasted_iota(jnp.int32, (256, 256), points_axis)
    place = lax.broadcasted_iota(jnp.int32, (256, 256), 1 - points_axis)
    value = entry(high, place >> 7, place & 31, point & 63)
    return jnp.where((point >> 6) == ((place >> 5) & 3), value, 0.0).astype(jnp.bfloat16)


def row_table(entry, high, points_axis):
    point = lax.broadcasted_iota(jnp.int32, (128, 128), points_axis)
    place = lax.broadcasted_iota(jnp.int32, (128, 128), 1 - points_axis)
    part = (place >> 3) * 4 + (place & 3)
    value = entry(high, part >> 5, part & 31, point & 63)
    return jnp.where((point >> 6) == ((place >> 2) & 1), value, 0.0).astype(jnp.bfloat16)


def split(values):
    high = values.astype(jnp.bfloat16)
    low = (values - high.astype(jnp.float32)).astype(jnp.bfloat16)
    return high, low


def dot(left, right):
    return jnp.dot(left, right, preferred_element_type=jnp.float32)


def roll_lanes(values):
    return jnp.concatenate(
        [pltpu.roll(values[:, :128], 96, 1), pltpu.roll(values[:, 128:], 96, 1)], axis=1
    )


def swap_halves(first, second):
    front = lax.broadcasted_iota(jnp.int32, first.shape, 1) < 64
    return (
        jnp.where(front, first, pltpu.roll(second, 64, 1)),
        jnp.where(front, pltpu.roll(first, 64, 1), second),
    )


def lanes_product(even, odd, table):
    even_high, even_low = split(even)
    odd_high, odd_low = split(odd)
    out = dot(jnp.concatenate([even_high, even_low, odd_high, odd_low], axis=0), table)
    return out[:128] + out[128:256], out[256:384] + out[384:]


def rows_product(table, values):
    high, low = split(values)
    return dot(table, high) + dot(table, low)


def offsets_of(levels_ref, grid):
    return [levels_ref[axis, grid] - LOWEST[axis] for axis in range(4)]


def cover_of(offsets, b, c, d):
    _, second, third, fourth = offsets
    covered = (1 - b + b * second) * (1 - c + c * third) * (1 - d + d * fourth)
    return covered, covered * ((b * (1 + third) + c) * (1 + fourth) + d)


def own_grid():
    return lax.axis_index("half") * 8 + lax.axis_index("grid")


def blocks_of(offsets, slot):
    _, second, third, fourth = offsets
    d_at = (slot % 2) * fourth
    rest = slot + fourth * (slot // 2 - slot)
    c_at = (rest % 2) * third
    rest = rest + third * (rest // 2 - rest)
    return jnp.where(rest <= second, rest * 4 + c_at * 2 + d_at, 0)


def lower(offsets, x_ref, held, blocks_ref):
    _, b_high, c_high, d_high = offsets
    lane = lane_table(down_entry, d_high, 0)
    row = row_table(down_entry, b_high, 1)
    fine = c_high == 1

    def tile(i, j):
        t = i + 8 * j
        u = i % 4 + 4 * j
        return jnp.where(
            fine, x_ref[:, t * 128 : t * 128 + 128], x_ref[:, u * 128 : u * 128 + 128]
        )

    for i in range(8):
        even01, odd01 = swap_halves(tile(i, 0), tile(i, 1))
        even23, odd23 = swap_halves(tile(i, 2), tile(i, 3))
        held[i], held[8 + i] = lanes_product(
            jnp.concatenate([even01, even23], axis=1),
            jnp.concatenate([odd01, odd23], axis=1),
            lane,
        )
    for m in range(7, -1, -1):
        held[16 + m] = jnp.where(fine, held[m], held[m // 2 + 8 * (m % 2)])
    for m in range(8):
        after = held[17 + m] if m < 7 else roll_lanes(held[16])
        held[8 + m] = held[8 + m] - 0.5 * (held[16 + m] + after)
    for c in range(2):
        for m in range(8):
            out = rows_product(row, held[16 - 8 * c + m])
            for b in range(2):
                for d in range(2):
                    for half in range(2):
                        start = b * 64 + half * 32
                        blocks_ref[half * 8 + m, b * 4 + c * 2 + d] = out[
                            start : start + 32, d * 128 : d * 128 + 128
                        ]


def backward_kernel(levels_ref, recv_ref, out_ref, held):
    offsets = offsets_of(levels_ref, own_grid())
    first, b_high, c_high, d_high = offsets
    inside = lax.axis_index("dom") < lax.shift_left(8, first)

    @pl.when(jnp.logical_not(inside))
    def _():
        out_ref[...] = jnp.zeros_like(out_ref)

    @pl.when(inside)
    def _():
        lane = lane_table(up_entry, d_high, 1)
        row = row_table(up_entry, b_high, 0)

        def rows(c, m):
            columns = []
            for d in range(2):
                parts = []
                for b in range(2):
                    covered, slot = cover_of(offsets, b, c, d)
                    for half in range(2):
                        for group in range(4):
                            part = recv_ref[group, half * 8 + m, slot]
                            parts.append(jnp.where(covered == 1, part, 0.0))
                columns.append(jnp.concatenate(parts, axis=0))
            held[c * 8 + m] = rows_product(row, jnp.concatenate(columns, axis=1))

        def step(i, count, even, odd):
            even, odd = lanes_product(even, odd, lane)
            tiles = swap_halves(even[:, :128], odd[:, :128]) + swap_halves(
                even[:, 128:], odd[:, 128:]
            )
            for j in range(4):
                t = i + j * count
                out_ref[:, t * 128 : t * 128 + 128] = tiles[j]

        for m in range(8):
            rows(0, m)

        @pl.when(c_high == 1)
        def _():
            for m in range(8):
                rows(1, m)
            for m in range(8):
                after = held[m + 1] if m < 7 else roll_lanes(held[0])
                step(m, 8, held[m], held[8 + m] + 0.5 * (held[m] + after))

        @pl.when(c_high == 0)
        def _():
            for i in range(4):
                step(i, 4, held[2 * i], held[2 * i + 1])
            out_ref[:, 2048:] = jnp.zeros((128, 2048), jnp.float32)


def weigh(levels_ref, weight_ref):
    guard = 0x8888
    packed = []
    for grid in range(16):
        first, second, third, fourth = offsets_of(levels_ref, grid)
        packed.append(first + 16 * second + 256 * third + 4096 * fourth)
    rows = lax.broadcasted_iota(jnp.int32, (16, 128), 0)
    corner = lax.broadcasted_iota(jnp.int32, (16, 128), 1)
    bits = [lax.shift_right_logical(corner, place) & 1 for place in range(4)]
    raised = bits[0] + 16 * bits[1] + 256 * bits[2] + 4096 * bits[3]
    for grid in range(16):
        raised = raised + jnp.where(rows == grid, packed[grid], 0)
    count = jnp.zeros((16, 128), jnp.int32)
    for grid in range(16):
        above = ((packed[grid] + guard) - raised) & guard
        count = count + jnp.where(above == guard, 1, 0)
    parity = 1 - 2 * ((bits[0] + bits[1] + bits[2] + bits[3]) & 1)
    signed = jnp.where((count > 0) & (corner < 16), parity, 0).astype(jnp.float32)
    total = jnp.sum(signed, axis=1, keepdims=True)
    weight_ref[...] = jnp.broadcast_to(total, (16, 128))


def exchange_kernel(levels_ref, x_ref, out_ref, *scratch):
    (
        r1,
        acc,
        r3,
        relayed,
        r2,
        o2,
        s2,
        weight_ref,
        slot_ref,
        coef_ref,
        pick_ref,
        send1,
        recv1,
        send2,
        recv2,
        send3,
        recv3,
        send4,
        recv4,
        sendr,
        recvr,
        sendf,
        recvf,
        own,
        send_ref,
        held,
        blocks_ref,
        here,
    ) = [scratch[4 * i : 4 * i + 4] for i in range(4)] + list(scratch[16:])
    half = lax.axis_index("half")
    line = lax.axis_index("grid")
    me = half * 8 + line
    dom = lax.axis_index("dom")
    far = dom // 16
    mine = dom % 4
    my_e = dom // 4

    for s in range(8):
        r2[s, 2] = jnp.zeros((8, 128), jnp.float32)

    barrier = pltpu.get_barrier_semaphore()

    def greet_group(k, _):
        peer = (me + k) % 16
        pl.semaphore_signal(
            barrier, inc=1, device_id={"half": peer // 8, "grid": peer % 8}, device_id_type=MESH
        )
        return 0

    def greet_near(k, _):
        pl.semaphore_signal(
            barrier, inc=1, device_id={"dom": (dom + k) % 32}, device_id_type=MESH
        )
        return 0

    def greet_far(k, _):
        pl.semaphore_signal(
            barrier, inc=1, device_id={"dom": 16 + (dom + k) % 16}, device_id_type=MESH
        )
        return 0

    def answer(k, _):
        pl.semaphore_signal(
            here, inc=1, device_id={"dom": (dom + k) % 16}, device_id_type=MESH
        )
        return 0

    lax.fori_loop(1, 16, greet_group, 0)

    @pl.when(far == 0)
    def _():
        lax.fori_loop(1, 32, greet_near, 0)

    @pl.when(far == 1)
    def _():
        lax.fori_loop(1, 16, greet_far, 0)

    offsets = offsets_of(levels_ref, me)
    lower(offsets, x_ref, held, blocks_ref)
    places = [blocks_of(offsets, slot) for slot in range(8)]

    def pack(c):
        def one(target, _):
            for slot in range(8):
                send_ref[c, target, slot] = blocks_ref[target, places[slot], pl.ds(8 * c, 8), :]
            return 0

        lax.fori_loop(0, 16, one, 0)

    pack(0)

    @pl.when(far == 0)
    def _():
        pl.semaphore_wait(barrier, 30)

    @pl.when(far == 1)
    def _():
        pl.semaphore_wait(barrier, 46)
        lax.fori_loop(0, 16, answer, 0)


    def sized(key, act):
        for option in range(3):

            @pl.when(key == option)
            def _():
                act(8 >> option)

    def copy1(c, source, peer, count):
        return pltpu.make_async_remote_copy(
            src_ref=send_ref.at[c, peer, pl.ds(0, count)],
            dst_ref=r1[c].at[source, pl.ds(0, count)],
            send_sem=send1.at[c, peer],
            recv_sem=recv1.at[c, source],
            device_id={"half": peer // 8, "grid": peer % 8},
            device_id_type=MESH,
        )

    def shared(source, owner_at, act):
        key = source // 8 + far
        direct = (owner_at // 8 == 0) | (source % 8 == owner_at % 8)

        @pl.when((key == 0) & direct)
        def _():
            act(8)

        @pl.when(((key == 0) & jnp.logical_not(direct)) | (key == 1))
        def _():
            act(4)

        @pl.when(key == 2)
        def _():
            act(2)

    def relay(c):
        return pltpu.make_async_remote_copy(
            src_ref=send_ref.at[c, pl.ds(8, 8), pl.ds(4, 4)],
            dst_ref=relayed[c],
            send_sem=sendr.at[c],
            recv_sem=recvr.at[c],
            device_id={"half": 1 - half},
            device_id_type=MESH,
        )

    def forward(c, source, to):
        return pltpu.make_async_remote_copy(
            src_ref=relayed[c].at[to],
            dst_ref=r1[c].at[source, pl.ds(4, 4)],
            send_sem=sendf.at[c, to],
            recv_sem=recvf.at[c, source],
            device_id={"grid": to},
            device_id_type=MESH,
        )

    gives = half + far == 0
    takes = (half == 1) & (far == 0)

    def pass_on(c):
        @pl.when(takes)
        def _():
            relay(c).wait_recv()

            def one(k, _):
                forward(c, line, (line + k) % 8).start()
                return 0

            lax.fori_loop(1, 8, one, 0)

    def ordered(k):
        step = (k - 1) // 2
        away = 4 + step // 2 - (step % 2) * (1 + 2 * (step // 2))
        return (half + k % 2) % 2 * 8 + (line + away) % 8

    def start1(c):
        def one(k, _):
            peer = ordered(k)
            shared(me, peer, lambda count: copy1(c, me, peer, count).start())
            return 0

        lax.fori_loop(1, 16, one, 0)

    def send(c):
        @pl.when(gives)
        def _():
            relay(c).start()

        start1(c)

    send(0)
    pack(1)
    send(1)
    pack(2)
    pack(3)


    weigh(levels_ref, weight_ref)
    near = 1 - far
    nearest = jnp.where(dom < 8, 1, 0)

    def table(i, _):
        grid = i // 8
        place = i % 8
        offsets = offsets_of(levels_ref, grid)
        first = offsets[0]
        covered, slot = cover_of(offsets, place // 4, place // 2 % 2, place % 2)
        is_two = jnp.where(first == 2, 1, 0)
        is_one = jnp.where(first == 1, 1, 0) * near
        is_zero = jnp.where(first == 0, 1, 0) * nearest
        slot_ref[i] = slot * (is_two + is_one + is_zero)
        coef_ref[3 * i] = (covered * is_two).astype(jnp.float32)
        coef_ref[3 * i + 1] = (covered * is_one).astype(jnp.float32)
        coef_ref[3 * i + 2] = (covered * is_zero).astype(jnp.float32)
        chosen = blocks_of(offsets, place)
        pick_ref[i] = chosen * 3 + is_one + 2 * is_zero
        return 0

    lax.fori_loop(0, 128, table, 0)

    def tiered(key, act):
        for option in range(3):

            @pl.when(key == option)
            def _():
                act(1 + option)

    def tiers(low, high):
        return (1 - low // 16) + jnp.where((low // 8) + (high // 4) == 0, 1, 0)

    def owner(c, e):
        return 4 * e + c

    def copy2(c, source, e, count):
        return pltpu.make_async_remote_copy(
            src_ref=acc[c].at[e, pl.ds(0, count)],
            dst_ref=r2.at[source, pl.ds(0, count)],
            send_sem=send2.at[c, e],
            recv_sem=recv2.at[source],
            device_id={"dom": owner(c, e)},
            device_id_type=MESH,
        )

    def copy3(c, e, peer, count):
        return pltpu.make_async_remote_copy(
            src_ref=o2.at[peer, pl.ds(0, count)],
            dst_ref=r3[c].at[pl.ds(e * 3, count)],
            send_sem=send3.at[peer],
            recv_sem=recv3.at[c, e],
            device_id={"dom": peer},
            device_id_type=MESH,
        )

    def copy4(c, source, peer, count):
        return pltpu.make_async_remote_copy(
            src_ref=s2.at[c, peer, pl.ds(0, count)],
            dst_ref=out_ref.at[c, source, pl.ds(0, count)],
            send_sem=send4.at[c, peer],
            recv_sem=recv4.at[c, source],
            device_id={"half": peer // 8, "grid": peer % 8},
            device_id_type=MESH,
        )

    def part(ref, kind, p):
        return ref[p // 2, kind, (p % 2) * 4 : (p % 2) * 4 + 4, :]

    def put(ref, kind, p, value):
        ref[p // 2, kind, (p % 2) * 4 : (p % 2) * 4 + 4, :] = value

    def joined(p):
        p = p % 32
        return part(r2, 0, 2 * p) + part(r2, 1, p)

    def coarse(q):
        q = q % 16
        return joined(2 * q) + part(r2, 2, q)

    def lift():
        for q in range(16):
            here = coarse(q)
            after = coarse(q + 1)
            middle = joined(2 * q + 1) - 0.5 * (joined(2 * q) + joined(2 * q + 2))
            put(o2, 2, q, here)
            put(o2, 1, 2 * q, here)
            put(o2, 1, 2 * q + 1, middle + 0.5 * (here + after))
        for s in range(32):
            here = part(o2, 1, s)
            after = part(o2, 1, (s + 1) % 32)
            fine = part(r2, 0, 2 * s + 1) - 0.5 * (
                part(r2, 0, 2 * s) + part(r2, 0, (2 * s + 2) % 64)
            )
            put(o2, 0, 2 * s, here)
            put(o2, 0, 2 * s + 1, fine + 0.5 * (here + after))

    def arrive(c):
        def wait1(k, _):
            source = (me + 16 - k) % 16
            shared(source, me, lambda count: copy1(c, source, source, count).wait_recv())

            @pl.when((source // 8 == 0) & takes & (source % 8 != line))
            def _():
                forward(c, source % 8, source % 8).wait_recv()

            return 0

        lax.fori_loop(1, 16, wait1, 0)

    def summed(c):
        def keep(slot, _):
            r1[c][me, slot] = send_ref[c, me, slot]
            return 0

        lax.fori_loop(0, 8, keep, 0)

        def add(block, _):
            sums = [jnp.zeros((8, 128), jnp.float32) for _ in range(2)]
            for source in range(16):
                at = source * 8 + block
                value = r1[c][source, slot_ref[at]] * weight_ref[pl.ds(source, 1), :]
                for kind in range(2):
                    sums[kind] = sums[kind] + value * coef_ref[3 * at + kind]
            for kind in range(2):
                acc[c][block, kind] = sums[kind]
            return 0

        lax.fori_loop(0, 8, add, 0)
        total = jnp.zeros((8, 128), jnp.float32)
        for source in range(16):
            value = r1[c][source, 0] * weight_ref[pl.ds(source, 1), :]
            total = total + value * coef_ref[3 * source * 8 + 2]
        acc[c][0, 2] = total

        def start2(k, _):
            e = (my_e + k) % 8
            peer = owner(c, e)

            @pl.when(peer != dom)
            def _():
                tiered(tiers(dom, peer), lambda count: copy2(c, dom, e, count).start())

            return 0

        lax.fori_loop(0, 8, start2, 0)

    def owned(c):
        @pl.when(mine == c)
        def _():
            for kind in range(2):
                r2[dom, kind] = acc[c][my_e, kind]

            @pl.when(my_e == 0)
            def _():
                r2[dom, 2] = acc[c][my_e, 2]

            def wait2(k, _):
                source = (dom + 32 - k) % 32
                tiered(
                    tiers(source, dom), lambda count: copy2(c, source, my_e, count).wait_recv()
                )
                return 0

            lax.fori_loop(1, 32, wait2, 0)
            lift()

            def start3(k, _):
                peer = (dom + k) % 32
                tiered(tiers(peer, dom), lambda count: copy3(c, my_e, peer, count).start())
                return 0

            lax.fori_loop(1, 32, start3, 0)
            r3[c][my_e * 3] = o2[dom, 0]

            @pl.when(far == 0)
            def _():
                r3[c][my_e * 3 + 1] = o2[dom, 1]

            @pl.when(my_e == 0)
            def _():
                r3[c][my_e * 3 + 2] = o2[dom, 2]

    def deliver(c):
        def wait3(k, _):
            e = (my_e + 8 - k) % 8
            peer = owner(c, e)

            @pl.when(peer != dom)
            def _():
                tiered(tiers(dom, peer), lambda count: copy3(c, e, dom, count).wait_recv())

            return 0

        lax.fori_loop(0, 8, wait3, 0)

        def fill(peer):
            for slot in range(8):
                s2[c, peer, slot] = r3[c][pick_ref[peer * 8 + slot]]

        def start4(k, _):
            peer = ordered(k)
            fill(peer)
            sized(peer // 8 + far, lambda count: copy4(c, me, peer, count).start())
            return 0

        lax.fori_loop(1, 16, start4, 0)
        fill(me)

    pass_on(0)
    send(2)
    pass_on(1)
    arrive(0)
    send(3)

    @pl.when(far == 0)
    def _():
        pl.semaphore_wait(here, 16)

    summed(0)
    pass_on(2)
    pass_on(3)
    owned(0)
    arrive(1)
    summed(1)
    deliver(0)
    owned(1)
    arrive(2)
    summed(2)
    deliver(1)
    owned(2)
    arrive(3)
    summed(3)
    deliver(2)
    owned(3)
    deliver(3)

    home = pltpu.make_async_copy(s2.at[:, me], out_ref.at[:, me], own)
    home.start()

    for c in range(4):

        def wait4(k, _):
            source = (me + 16 - k) % 16
            sized(half + far, lambda count: copy4(c, source, source, count).wait_recv())
            return 0

        lax.fori_loop(1, 16, wait4, 0)

    home.wait()

    def sent_group(k, _):
        peer = (me + k) % 16
        for c in range(4):
            shared(me, peer, lambda count: copy1(c, me, peer, count).wait_send())
            sized(peer // 8 + far, lambda count: copy4(c, me, peer, count).wait_send())
        return 0

    lax.fori_loop(1, 16, sent_group, 0)

    @pl.when(gives)
    def _():
        for c in range(4):
            relay(c).wait_send()

    @pl.when(takes)
    def _():
        def passed(k, _):
            for c in range(4):
                forward(c, line, (line + k) % 8).wait_send()
            return 0

        lax.fori_loop(1, 8, passed, 0)

    for c in range(4):

        def sent2(e, _):
            peer = owner(c, e)

            @pl.when(peer != dom)
            def _():
                tiered(tiers(dom, peer), lambda count: copy2(c, dom, e, count).wait_send())

            return 0

        lax.fori_loop(0, 8, sent2, 0)

    def sent3(k, _):
        peer = (dom + k) % 32
        tiered(tiers(peer, dom), lambda count: copy3(0, my_e, peer, count).wait_send())
        return 0

    lax.fori_loop(1, 32, sent3, 0)


def exchange(levels, values):
    dma = pltpu.SemaphoreType.DMA
    f32 = jnp.float32
    return pl.pallas_call(
        exchange_kernel,
        out_shape=jax.ShapeDtypeStruct((4, 16, 8, 8, 128), f32),
        in_specs=[
            pl.BlockSpec(memory_space=pltpu.SMEM),
            pl.BlockSpec(memory_space=pltpu.VMEM),
        ],
        out_specs=pl.BlockSpec(memory_space=pl.ANY),
        scratch_shapes=[pltpu.VMEM((16, 8, 8, 128), f32)] * 4
        + [pltpu.VMEM((8, 3, 8, 128), f32)] * 4
        + [pltpu.VMEM((24, 8, 128), f32)] * 4
        + [pltpu.VMEM((8, 4, 8, 128), f32)] * 4
        + [
            pltpu.VMEM((32, 3, 8, 128), f32),
            pltpu.VMEM((32, 3, 8, 128), f32),
            pltpu.VMEM((4, 16, 8, 8, 128), f32),
            pltpu.VMEM((16, 128), f32),
            pltpu.SMEM((128,), jnp.int32),
            pltpu.SMEM((384,), f32),
            pltpu.SMEM((128,), jnp.int32),
            dma((4, 16)),
            dma((4, 16)),
            dma((4, 8)),
            dma((32,)),
            dma((32,)),
            dma((4, 8)),
            dma((4, 16)),
            dma((4, 16)),
            dma((4,)),
            dma((4,)),
            dma((4, 8)),
            dma((4, 8)),
            dma,
            pltpu.VMEM((4, 16, 8, 8, 128), f32),
            pltpu.VMEM((24, 128, 256), f32),
            pltpu.VMEM((16, 8, 32, 128), f32),
            pltpu.SemaphoreType.REGULAR,
        ],
        compiler_params=pltpu.CompilerParams(
            collective_id=0, has_side_effects=True, vmem_limit_bytes=32 * 2**20
        ),
    )(levels, values)


def local_call(kernel, levels, values, out_shape):
    return pl.pallas_call(
        kernel,
        out_shape=jax.ShapeDtypeStruct(out_shape, jnp.float32),
        in_specs=[
            pl.BlockSpec(memory_space=pltpu.SMEM),
            pl.BlockSpec(memory_space=pltpu.VMEM),
        ],
        out_specs=pl.BlockSpec(memory_space=pltpu.VMEM),
        scratch_shapes=[pltpu.VMEM((16, 128, 256), jnp.float32)],
        compiler_params=pltpu.CompilerParams(vmem_limit_bytes=32 * 2**20),
    )(levels, values)


def per_device(grids, levels):
    turned = levels.T
    received = exchange(turned, grids.reshape(128, 4096))
    combined = local_call(backward_kernel, turned, received, (128, 4096))
    return combined.reshape(grids.shape)


def solution(mesh):
    return jax.shard_map(
        per_device,
        mesh=mesh,
        in_specs=(P(("half", "grid"), "dom", None, None), P()),
        out_specs=P(("half", "grid"), "dom", None, None),
        check_vma=False,
    )
```
